32 devices in a mesh: groups: 2 (over x), epoch: 4 (over y, core), space: 4 (over z).
Axes of the slice: x: 2, y: 2, z: 4, core: 2. Of those that a mesh axis runs over, the one named last changes fastest.
Arguments:
- slc_stack: bfloat16 [2, 32, 32, 960], P(None, ('epoch', 'space'), 'groups'), parts along dimension 2, may hold values from -45 to 45
Outputs:
- coherence: bfloat16 [2, 32, 32, 2048], P(None, 'epoch', None, ('groups', 'space')), parts along dimension 3
The draws below stay inside these ranges and needn't reach their ends.
There are 2 independent parts, one for each index of `groups`. The reference program is written for one: setup_inputs(seed, part) draws one part's arguments, and reference() takes and returns one part's arrays. A program takes and returns all parts, laid end to end along the dimension named above; each array names one. Nothing has to cross between parts.
All inputs are finite; a program needn't handle non-finite values.
Results may differ from the reference program's by a relative error of at most 0.001.
Values may be sent and summed in bfloat16 or wider, within the bound.
A program may use at most 128 MiB of HBM per device.

```python
import math
import jax
import jax.numpy as jnp
from jax import lax

E = 32
LC = 64
LOOKR = 5
LOOKC = 15
MARGIN = 2
ROWS = 16
COLS = 960


def draw_slc_stack(key, part):
    key_weight, key_common, key_amp, key_noise = jax.random.split(jax.random.fold_in(key, 11), 4)
    weights = jax.random.uniform(key_weight, (1, E, 1, 1), jnp.float32, 0.2, 1.5)
    common = jnp.clip(jax.random.normal(key_common, (2, 1, ROWS, COLS), jnp.float32), -6.0, 6.0)
    amplitude = jnp.exp(jax.random.uniform(key_amp, (1, 1, ROWS, COLS), jnp.float32, math.log(0.3), math.log(3.0)))
    noise = jnp.clip(jax.random.normal(key_noise, (2, E, ROWS, COLS), jnp.float32), -6.0, 6.0)
    return (amplitude * (weights * common + noise)).astype(jnp.bfloat16)


def setup_inputs(seed: int = 0, part: int = 0) -> dict:
    keys = jax.random.split(jax.random.key(seed), 2)
    own_keys = jax.random.split(jax.random.fold_in(keys[1], part), 2)
    return {
        "slc_stack": draw_slc_stack(jax.random.fold_in(jax.random.fold_in(keys[1], part), 71), part),
    }


def window_sums(values_in):
    row_count = values_in.shape[-2] - 2 * MARGIN
    col_count = values_in.shape[-1] // LOOKC
    folded = values_in.reshape(values_in.shape[:-1] + (col_count, LOOKC)).sum(-1)
    running = folded[..., 0:row_count, :]
    for offset in range(1, LOOKR):
        running = running + folded[..., offset:offset + row_count, :]
    return running

def powers_of(strip_data):
    real_part = strip_data[0].astype(jnp.float32)
    imag_part = strip_data[1].astype(jnp.float32)
    return window_sums(real_part * real_part + imag_part * imag_part) + 1e-06

def pair_coherence(left_strip, right_strip, left_power, right_power):
    left_re = left_strip[0].astype(jnp.float32)[:, None]
    left_im = left_strip[1].astype(jnp.float32)[:, None]
    right_re = right_strip[0].astype(jnp.float32)[None]
    right_im = right_strip[1].astype(jnp.float32)[None]
    cross_re = window_sums(left_re * right_re + left_im * right_im)
    cross_im = window_sums(left_im * right_re - left_re * right_im)
    inverse = lax.rsqrt(left_power[:, None] * right_power[None])
    return jnp.stack([cross_re * inverse, cross_im * inverse]).astype(jnp.bfloat16)

def reference(slc_stack):
    padded = jnp.pad(slc_stack, ((0, 0), (0, 0), (MARGIN, MARGIN), (0, 0)))
    power_all = powers_of(padded)

    def one_epoch(epoch_index):
        left_strip = lax.dynamic_slice_in_dim(padded, epoch_index, 1, 1)
        left_power = lax.dynamic_slice_in_dim(power_all, epoch_index, 1, 0)
        return pair_coherence(left_strip, padded, left_power, power_all)[:, 0]
    result = lax.map(one_epoch, jnp.arange(E, dtype=jnp.int32))
    return jnp.transpose(result, (1, 0, 2, 3, 4)).reshape(2, E, E, ROWS * LC)
```

```python
import functools

import jax
import jax.numpy as jnp
from jax import lax
from jax.experimental import pallas as pl
from jax.experimental.pallas import tpu as pltpu
from jax.sharding import PartitionSpec as P

LOOKR = 5
LOOKC = 15
MARGIN = 2
LANES = 128
MESH = pl.DeviceIdType.MESH
F32 = jnp.float32
BF16 = jnp.bfloat16


def iota(shape, axis):
    return lax.broadcasted_iota(jnp.int32, shape, axis)


def one_hot(hits):
    return jnp.where(hits, 1.0, 0.0).astype(BF16)


def kernel(dims, x_ref, out_ref, strips, parts, epochs, lefts, powers, coh, got, *sems):
    n_epoch, n_space, local, rows, cols, strip = dims
    send1, recv1, send2, recv2 = sems
    total = n_epoch * n_space * local
    block = n_space * local
    held = strip + 2 * MARGIN
    width = cols // n_epoch
    lane_pad = strips.shape[-1] // 2
    looks = width // LOOKC
    all_looks = cols // LOOKC
    lanes = block * looks
    my_i = lax.axis_index("epoch")
    my_j = lax.axis_index("space")
    me = my_i * n_space + my_j

    def epoch_peer(step):
        core = lax.rem(lax.rem(my_i, 2) + step % 2, 2)
        return lax.rem(my_i // 2 + step // 2, n_epoch // 2) * 2 + core

    def epoch_source(step):
        core = lax.rem(lax.rem(my_i, 2) + step % 2, 2)
        return lax.rem(my_i // 2 + n_epoch // 2 - step // 2, n_epoch // 2) * 2 + core

    steps = [
        (a, b)
        for b in reversed(range(n_space))
        for a in reversed(range(n_epoch))
        if a or b
    ]

    barrier = pltpu.get_barrier_semaphore()
    for a, b in steps:
        pl.semaphore_signal(
            barrier,
            inc=1,
            device_id={"epoch": epoch_peer(a), "space": lax.rem(my_j + b, n_space)},
            device_id_type=MESH,
        )

    cut = (n_space * held * local, local * rows)
    at = iota(cut, 0)
    strip_of, row_of, own_of = at // (held * local), (at // local) % held, at % local
    pick_own, pick_row = iota(cut, 1) // rows, iota(cut, 1) % rows
    pick = one_hot((pick_own == own_of) & (pick_row == strip_of * strip + row_of - MARGIN))
    for k in range(2):
        picked = jnp.dot(pick, x_ref[k].reshape(local * rows, cols), preferred_element_type=F32)
        for i in range(n_epoch):
            piece = picked[:, i * width : (i + 1) * width]
            if lane_pad > width:
                piece = jnp.concatenate(
                    [piece, jnp.zeros((piece.shape[0], lane_pad - width), F32)], axis=1
                )
            piece = piece.astype(BF16)
            for j in range(n_space):
                strips[i * n_space + j, :, k * lane_pad : (k + 1) * lane_pad] = piece[
                    j * held * local : (j + 1) * held * local
                ]

    pl.semaphore_wait(barrier, len(steps))

    def first_copy(slot, to_i, to_j, source):
        return pltpu.make_async_remote_copy(
            src_ref=strips.at[to_i * n_space + to_j],
            dst_ref=parts.at[source],
            send_sem=send1.at[slot],
            recv_sem=recv1.at[source],
            device_id={"epoch": to_i, "space": to_j},
            device_id_type=MESH,
        )

    sent = []
    for slot, (a, b) in enumerate(steps):
        copy = first_copy(slot, epoch_peer(a), lax.rem(my_j + b, n_space), me)
        copy.start()
        sent.append(copy)
    parts[me] = strips[me]
    for slot, (a, b) in enumerate(steps):
        from_i, from_j = epoch_source(a), lax.rem(my_j + n_space - b, n_space)
        first_copy(slot, from_i, from_j, from_i * n_space + from_j).wait_recv()

    size = total * held
    to, fro = iota((size, size), 0), iota((size, size), 1)
    order = one_hot(
        (to // total == (fro // local) % held)
        & (to % total == fro // (held * local) * local + fro % local)
    )
    arrived = parts[...]
    if (held * local) % 16:
        arrived = arrived.astype(F32).reshape(size, 2 * lane_pad).astype(BF16)
    else:
        arrived = arrived.reshape(size, 2 * lane_pad)
    by_row = jnp.dot(order, arrived, preferred_element_type=F32)
    epochs[...] = by_row
    re, im = by_row[:, :lane_pad], by_row[:, lane_pad:]
    turned = jnp.concatenate([-im, re], axis=1).astype(BF16)
    plain = by_row.astype(BF16)
    for row in range(held):
        lefts[row, :total] = plain[row * total : (row + 1) * total]
        lefts[row, total:] = turned[row * total : (row + 1) * total]

    square = (re * re + im * im).reshape(held, total, lane_pad)
    summed = [
        functools.reduce(lambda p, q: p + q, [square[r + d] for d in range(LOOKR)])
        for r in range(strip)
    ]
    summed = jnp.concatenate(summed, axis=0)
    look = iota((lane_pad, lanes), 1) % looks
    col = iota((lane_pad, lanes), 0)
    fold = jnp.where((col >= look * LOOKC) & (col < look * LOOKC + LOOKC), 1.0, 0.0)
    power = jnp.dot(summed, fold, preferred_element_type=F32, precision=lax.Precision.HIGHEST)
    power = power + 1e-06
    for r in range(strip):
        powers[r] = power[r * total : (r + 1) * total]

    window = iota((1, looks, 2 * lane_pad), 1) * LOOKC
    place = iota((1, looks, 2 * lane_pad), 2) % lane_pad
    inside = (place >= window) & (place < window + LOOKC)
    own_lane = iota((block, lanes), 1) // looks == iota((block, lanes), 0)

    def second_copy(slot, to_i, source):
        return pltpu.make_async_remote_copy(
            src_ref=coh.at[slot],
            dst_ref=got.at[source],
            send_sem=send2.at[slot],
            recv_sem=recv2.at[source],
            device_id={"epoch": to_i},
            device_id_type=MESH,
        )

    for step in reversed(range(n_epoch)):
        to_i = epoch_peer(step)
        first = to_i * block
        grams = []
        for row in range(held):
            start = row * total + first
            if block % 8 == 0:
                start = pl.multiple_of(start, 8)
            mine = epochs[pl.ds(start, block), :]
            masked = jnp.where(inside, mine[:, None, :], 0.0).astype(BF16)
            grams.append(
                lax.dot_general(
                    lefts[row],
                    masked.reshape(lanes, 2 * lane_pad),
                    (((1,), (1,)), ((), ())),
                    preferred_element_type=F32,
                )
            )
        for r in range(strip):
            cross = functools.reduce(lambda p, q: p + q, grams[r : r + LOOKR])
            left = powers[r, pl.ds(pl.multiple_of(first, 8) if block % 8 == 0 else first, block), :]
            left = jnp.sum(jnp.where(own_lane, left, 0.0), axis=0, keepdims=True)
            inverse = lax.rsqrt(left * powers[r])
            value = jnp.concatenate(
                [cross[:total] * inverse, cross[total:] * inverse], axis=0
            ).astype(BF16)
            if step:
                coh[step, r] = value
            else:
                got[my_i, r] = value
        if step:
            copy = second_copy(step, to_i, my_i)
            copy.start()
            sent.append(copy)

    for step in reversed(range(1, n_epoch)):
        from_i = epoch_source(step)
        second_copy(step, from_i, from_i).wait_recv()

    if lanes == LANES and (strip * n_epoch) % block == 0 and block & (block - 1) == 0:
        spot = iota((2 * total, lanes), 1) // looks
        for half in range(strip * n_epoch // block):
            tiles = []
            for t in range(half * block, (half + 1) * block):
                tiles.append(got[t % n_epoch, t // n_epoch].astype(F32))
            bit = 1
            while bit < block:
                low = (spot // bit) % 2 == 0
                turned_tiles = list(tiles)
                for t in range(block):
                    if t & bit:
                        continue
                    one, two = tiles[t], tiles[t + bit]
                    turned_tiles[t] = jnp.where(low, one, pltpu.roll(two, bit * looks, 1))
                    turned_tiles[t + bit] = jnp.where(
                        low, pltpu.roll(one, lanes - bit * looks, 1), two
                    )
                tiles = turned_tiles
                bit *= 2
            for e in range(block):
                value = tiles[e].astype(BF16)
                for k in range(2):
                    out_ref[k, e, :, half * lanes : (half + 1) * lanes] = value[
                        k * total : (k + 1) * total
                    ]
    else:
        shape = (lanes, strip * all_looks)
        fro_e, fro_c, goal = iota(shape, 0) // looks, iota(shape, 0) % looks, iota(shape, 1)
        for e in range(block):

            def add(i, acc):
                for r in range(strip):
                    spread = one_hot((fro_e == e) & (goal == r * all_looks + i * looks + fro_c))
                    acc = acc + jnp.dot(got[i, r], spread, preferred_element_type=F32)
                return acc

            value = lax.fori_loop(0, n_epoch, add, jnp.zeros((2 * total, shape[1]), F32))
            value = value.astype(BF16)
            for k in range(2):
                out_ref[k, e] = value[k * total : (k + 1) * total]

    for copy in sent:
        copy.wait_send()


def per_device(slc_stack):
    n_epoch, n_space = lax.axis_size("epoch"), lax.axis_size("space")
    _, local, rows, cols = slc_stack.shape
    strip = rows // n_space
    held = strip + 2 * MARGIN
    total = n_epoch * n_space * local
    block = n_space * local
    width = cols // n_epoch
    lane_pad = -(-width // LANES) * LANES
    lanes = block * (width // LOOKC)
    sources = n_epoch * n_space
    dims = (n_epoch, n_space, local, rows, cols, strip)
    vmem = pl.BlockSpec(memory_space=pltpu.VMEM)
    return pl.pallas_call(
        functools.partial(kernel, dims),
        out_shape=jax.ShapeDtypeStruct((2, block, total, strip * (cols // LOOKC)), BF16),
        in_specs=[vmem],
        out_specs=vmem,
        scratch_shapes=[
            pltpu.VMEM((sources, held * local, 2 * lane_pad), BF16),
            pltpu.VMEM((sources, held * local, 2 * lane_pad), BF16),
            pltpu.VMEM((held * total, 2 * lane_pad), F32),
            pltpu.VMEM((held, 2 * total, 2 * lane_pad), BF16),
            pltpu.VMEM((strip, total, lanes), F32),
            pltpu.VMEM((n_epoch, strip, 2 * total, lanes), BF16),
            pltpu.VMEM((n_epoch, strip, 2 * total, lanes), BF16),
            pltpu.SemaphoreType.DMA((sources - 1,)),
            pltpu.SemaphoreType.DMA((sources,)),
            pltpu.SemaphoreType.DMA((n_epoch,)),
            pltpu.SemaphoreType.DMA((n_epoch,)),
        ],
        compiler_params=pltpu.CompilerParams(
            collective_id=0, has_side_effects=True, vmem_limit_bytes=48 * 1024 * 1024
        ),
        cost_estimate=pl.CostEstimate(flops=10**9, bytes_accessed=10**6, transcendentals=0),
    )(slc_stack)


def solution(mesh):
    in_specs = (P(None, ("epoch", "space"), "groups", None),)
    out_specs = P(None, "epoch", None, ("groups", "space"))
    return jax.shard_map(
        per_device, mesh=mesh, in_specs=in_specs, out_specs=out_specs, check_vma=False
    )
```

```python
import functools

import jax
import jax.numpy as jnp
from jax import lax
from jax.experimental import pallas as pl
from jax.experimental.pallas import tpu as pltpu
from jax.sharding import PartitionSpec as P

LOOKR = 5
LOOKC = 15
MARGIN = 2
LANES = 128
MESH = pl.DeviceIdType.MESH
F32 = jnp.float32
BF16 = jnp.bfloat16


def iota(shape, axis):
    return lax.broadcasted_iota(jnp.int32, shape, axis)


def one_hot(hits):
    return jnp.where(hits, 1.0, 0.0).astype(BF16)


def over(value, by):
    return value >> (by.bit_length() - 1) if by & (by - 1) == 0 else lax.div(value, by)


def rest(value, by):
    return value & (by - 1) if by & (by - 1) == 0 else lax.rem(value, by)


def kernel(dims, x_hbm, got, x_ref, strips, parts, epochs, lefts, powers, coh, order, fold, *sems):
    n_epoch, n_space, local, rows, cols, strip = dims
    load, send1, recv1, send2, recv2 = sems
    total = n_epoch * n_space * local
    block = n_space * local
    held = strip + 2 * MARGIN
    width = cols // n_epoch
    lane_pad = strips.shape[-1] // 2
    looks = width // LOOKC
    lanes = block * looks
    my_i = lax.axis_index("epoch")
    my_j = lax.axis_index("space")
    me = my_i * n_space + my_j

    def epoch_peer(step):
        core = lax.rem(lax.rem(my_i, 2) + step % 2, 2)
        return lax.rem(my_i // 2 + step // 2, n_epoch // 2) * 2 + core

    def epoch_source(step):
        core = lax.rem(lax.rem(my_i, 2) + step % 2, 2)
        return lax.rem(my_i // 2 + n_epoch // 2 - step // 2, n_epoch // 2) * 2 + core

    steps = [
        (a, b)
        for b in reversed(range(n_space))
        for a in reversed(range(n_epoch))
        if a or b
    ]

    loading = pltpu.make_async_copy(x_hbm, x_ref, load)
    loading.start()
    barrier = pltpu.get_barrier_semaphore()
    for a, b in steps:
        pl.semaphore_signal(
            barrier,
            inc=1,
            device_id={"epoch": epoch_peer(a), "space": lax.rem(my_j + b, n_space)},
            device_id_type=MESH,
        )

    cut = (n_space * held * local, local * rows)
    at = iota(cut, 0)
    strip_of = over(at, held * local)
    row_of, own_of = rest(over(at, local), held), rest(at, local)
    pick_own, pick_row = over(iota(cut, 1), rows), rest(iota(cut, 1), rows)
    pick = one_hot((pick_own == own_of) & (pick_row == strip_of * strip + row_of - MARGIN))
    loading.wait()
    for k in range(2):
        picked = jnp.dot(pick, x_ref[k].reshape(local * rows, cols), preferred_element_type=F32)
        for i in range(n_epoch):
            piece = picked[:, i * width : (i + 1) * width]
            if lane_pad > width:
                piece = jnp.concatenate(
                    [piece, jnp.zeros((piece.shape[0], lane_pad - width), F32)], axis=1
                )
            piece = piece.astype(BF16)
            for j in range(n_space):
                strips[i * n_space + j, :, k * lane_pad : (k + 1) * lane_pad] = piece[
                    j * held * local : (j + 1) * held * local
                ]

    pl.semaphore_wait(barrier, len(steps))

    def first_copy(slot, to_i, to_j, source):
        return pltpu.make_async_remote_copy(
            src_ref=strips.at[to_i * n_space + to_j],
            dst_ref=parts.at[source],
            send_sem=send1.at[slot],
            recv_sem=recv1.at[source],
            device_id={"epoch": to_i, "space": to_j},
            device_id_type=MESH,
        )

    sent = []
    for slot, (a, b) in enumerate(steps):
        copy = first_copy(slot, epoch_peer(a), lax.rem(my_j + b, n_space), me)
        copy.start()
        sent.append(copy)
    parts[me] = strips[me]
    size = total * held
    to, fro = iota((size, size), 0), iota((size, size), 1)
    source_row = rest(over(fro, local), held)
    source_epoch = over(fro, held * local) * local + rest(fro, local)
    order[...] = one_hot((over(to, total) == source_row) & (rest(to, total) == source_epoch))
    look = rest(iota((lane_pad, lanes), 1), looks) * LOOKC
    col = iota((lane_pad, lanes), 0)
    fold[...] = jnp.where((col >= look) & (col < look + LOOKC), 1.0, 0.0)
    for slot, (a, b) in enumerate(steps):
        from_i, from_j = epoch_source(a), lax.rem(my_j + n_space - b, n_space)
        first_copy(slot, from_i, from_j, from_i * n_space + from_j).wait_recv()

    arrived = parts[...]
    if (held * local) % 16:
        arrived = arrived.astype(F32).reshape(size, 2 * lane_pad).astype(BF16)
    else:
        arrived = arrived.reshape(size, 2 * lane_pad)
    by_row = jnp.dot(order[...], arrived, preferred_element_type=F32)
    epochs[...] = by_row
    re, im = by_row[:, :lane_pad], by_row[:, lane_pad:]
    turned = jnp.concatenate([-im, re], axis=1).astype(BF16)
    plain = by_row.astype(BF16)
    for row in range(held):
        lefts[row, :total] = plain[row * total : (row + 1) * total]
        lefts[row, total:] = turned[row * total : (row + 1) * total]

    square = (re * re + im * im).reshape(held, total, lane_pad)
    summed = [
        functools.reduce(lambda p, q: p + q, [square[r + d] for d in range(LOOKR)])
        for r in range(strip)
    ]
    summed = jnp.concatenate(summed, axis=0)
    power = jnp.dot(summed, fold[...], preferred_element_type=F32, precision=lax.Precision.HIGHEST)
    power = power + 1e-06
    for r in range(strip):
        powers[r] = power[r * total : (r + 1) * total]

    window = iota((1, looks, 2 * lane_pad), 1) * LOOKC
    place = iota((1, looks, 2 * lane_pad), 2)
    place = jnp.where(place < lane_pad, place, place - lane_pad)
    inside = (place >= window) & (place < window + LOOKC)
    own_lane = over(iota((block, lanes), 1), looks) == iota((block, lanes), 0)

    def second_copy(slot, to_i, source):
        return pltpu.make_async_remote_copy(
            src_ref=coh.at[slot],
            dst_ref=got.at[source],
            send_sem=send2.at[slot],
            recv_sem=recv2.at[source],
            device_id={"epoch": to_i},
            device_id_type=MESH,
        )

    for step in reversed(range(n_epoch)):
        to_i = epoch_peer(step)
        first = to_i * block
        grams = []
        for row in range(held):
            start = row * total + first
            if block % 8 == 0:
                start = pl.multiple_of(start, 8)
            mine = epochs[pl.ds(start, block), :]
            masked = jnp.where(inside, mine[:, None, :], 0.0).astype(BF16)
            grams.append(
                lax.dot_general(
                    lefts[row],
                    masked.reshape(lanes, 2 * lane_pad),
                    (((1,), (1,)), ((), ())),
                    preferred_element_type=F32,
                )
            )
        for r in range(strip):
            cross = functools.reduce(lambda p, q: p + q, grams[r : r + LOOKR])
            left = powers[r, pl.ds(pl.multiple_of(first, 8) if block % 8 == 0 else first, block), :]
            left = jnp.sum(jnp.where(own_lane, left, 0.0), axis=0, keepdims=True)
            inverse = lax.rsqrt(left * powers[r])
            value = jnp.concatenate(
                [cross[:total] * inverse, cross[total:] * inverse], axis=0
            ).astype(BF16)
            if step:
                coh[step, r] = value
            else:
                got[my_i, r] = value
        if step:
            copy = second_copy(step, to_i, my_i)
            copy.start()
            sent.append(copy)

    for step in reversed(range(1, n_epoch)):
        from_i = epoch_source(step)
        second_copy(step, from_i, from_i).wait_recv()

    for copy in sent:
        copy.wait_send()


def spread_kernel(dims, got, out_hbm, out_ref, sem):
    n_epoch, block, total, strip, all_looks = dims
    looks = all_looks // n_epoch
    lanes = block * looks
    if lanes == LANES and (strip * n_epoch) % block == 0 and block & (block - 1) == 0:
        spot = over(iota((2 * total, lanes), 1), looks)
        copies = []
        for half in range(strip * n_epoch // block):
            tiles = []
            for t in range(half * block, (half + 1) * block):
                tiles.append(got[t % n_epoch, t // n_epoch].astype(F32))
            bit = 1
            while bit < block:
                low = spot & bit == 0
                turned_tiles = list(tiles)
                for t in range(block):
                    if t & bit:
                        continue
                    one, two = tiles[t], tiles[t + bit]
                    turned_tiles[t] = jnp.where(low, one, pltpu.roll(two, bit * looks, 1))
                    turned_tiles[t + bit] = jnp.where(
                        low, pltpu.roll(one, lanes - bit * looks, 1), two
                    )
                tiles = turned_tiles
                bit *= 2
            for e in range(block):
                value = tiles[e].astype(BF16)
                for k in range(2):
                    out_ref[k, e, :, half * lanes : (half + 1) * lanes] = value[
                        k * total : (k + 1) * total
                    ]
            side = pl.ds(half * lanes, lanes)
            copies.append(
                pltpu.make_async_copy(
                    out_ref.at[:, :, :, side], out_hbm.at[:, :, :, side], sem.at[half]
                )
            )
            copies[-1].start()
        for copy in copies:
            copy.wait()
    else:
        shape = (lanes, strip * all_looks)
        fro_e, fro_c, goal = iota(shape, 0) // looks, iota(shape, 0) % looks, iota(shape, 1)
        for e in range(block):

            def add(i, acc):
                for r in range(strip):
                    spread = one_hot((fro_e == e) & (goal == r * all_looks + i * looks + fro_c))
                    acc = acc + jnp.dot(got[i, r], spread, preferred_element_type=F32)
                return acc

            value = lax.fori_loop(0, n_epoch, add, jnp.zeros((2 * total, shape[1]), F32))
            value = value.astype(BF16)
            for k in range(2):
                out_ref[k, e] = value[k * total : (k + 1) * total]
        whole = pltpu.make_async_copy(out_ref, out_hbm, sem.at[0])
        whole.start()
        whole.wait()


def per_device(slc_stack):
    n_epoch, n_space = lax.axis_size("epoch"), lax.axis_size("space")
    _, local, rows, cols = slc_stack.shape
    strip = rows // n_space
    held = strip + 2 * MARGIN
    total = n_epoch * n_space * local
    block = n_space * local
    width = cols // n_epoch
    lane_pad = -(-width // LANES) * LANES
    lanes = block * (width // LOOKC)
    sources = n_epoch * n_space
    dims = (n_epoch, n_space, local, rows, cols, strip)
    all_looks = cols // LOOKC
    vmem = pl.BlockSpec(memory_space=pltpu.VMEM)
    hbm = pl.BlockSpec(memory_space=pl.ANY)
    got = pl.pallas_call(
        functools.partial(kernel, dims),
        out_shape=jax.ShapeDtypeStruct((n_epoch, strip, 2 * total, lanes), BF16),
        in_specs=[hbm],
        out_specs=vmem,
        scratch_shapes=[
            pltpu.VMEM(slc_stack.shape, BF16),
            pltpu.VMEM((sources, held * local, 2 * lane_pad), BF16),
            pltpu.VMEM((sources, held * local, 2 * lane_pad), BF16),
            pltpu.VMEM((held * total, 2 * lane_pad), F32),
            pltpu.VMEM((held, 2 * total, 2 * lane_pad), BF16),
            pltpu.VMEM((strip, total, lanes), F32),
            pltpu.VMEM((n_epoch, strip, 2 * total, lanes), BF16),
            pltpu.VMEM((held * total, held * total), BF16),
            pltpu.VMEM((lane_pad, lanes), F32),
            pltpu.SemaphoreType.DMA(()),
            pltpu.SemaphoreType.DMA((sources - 1,)),
            pltpu.SemaphoreType.DMA((sources,)),
            pltpu.SemaphoreType.DMA((n_epoch,)),
            pltpu.SemaphoreType.DMA((n_epoch,)),
        ],
        compiler_params=pltpu.CompilerParams(
            collective_id=0, has_side_effects=True, vmem_limit_bytes=48 * 1024 * 1024
        ),
        cost_estimate=pl.CostEstimate(flops=10**9, bytes_accessed=10**6, transcendentals=0),
    )(slc_stack)
    out = jax.ShapeDtypeStruct((2, block, total, strip * all_looks), BF16)
    return pl.pallas_call(
        functools.partial(spread_kernel, (n_epoch, block, total, strip, all_looks)),
        out_shape=out,
        in_specs=[vmem],
        out_specs=hbm,
        scratch_shapes=[
            pltpu.VMEM(out.shape, BF16),
            pltpu.SemaphoreType.DMA((max(1, strip * n_epoch // block),)),
        ],
        compiler_params=pltpu.CompilerParams(vmem_limit_bytes=32 * 1024 * 1024),
    )(got)


def solution(mesh):
    in_specs = (P(None, ("epoch", "space"), "groups", None),)
    out_specs = P(None, "epoch", None, ("groups", "space"))
    return jax.shard_map(
        per_device, mesh=mesh, in_specs=in_specs, out_specs=out_specs, check_vma=False
    )
```

```python
import functools

import jax
import jax.numpy as jnp
from jax import lax
from jax.experimental import pallas as pl
from jax.experimental.pallas import tpu as pltpu
from jax.sharding import PartitionSpec as P

LOOKR = 5
LOOKC = 15
MARGIN = 2
LANES = 128
MESH = pl.DeviceIdType.MESH
F32 = jnp.float32
BF16 = jnp.bfloat16


def iota(shape, axis):
    return lax.broadcasted_iota(jnp.int32, shape, axis)


def one_hot(hits):
    return jnp.where(hits, 1.0, 0.0).astype(BF16)


def over(value, by):
    return value >> (by.bit_length() - 1) if by & (by - 1) == 0 else lax.div(value, by)


def rest(value, by):
    return value & (by - 1) if by & (by - 1) == 0 else lax.rem(value, by)


def kernel(dims, x_hbm, got, x_ref, strips, parts, epochs, lefts, powers, coh, order, fold, *sems):
    n_epoch, n_space, local, rows, cols, strip = dims
    load, send1, recv1, send2, recv2 = sems
    total = n_epoch * n_space * local
    block = n_space * local
    held = strip + 2 * MARGIN
    width = cols // n_epoch
    lane_pad = strips.shape[-1] // 2
    looks = width // LOOKC
    lanes = block * looks
    my_i = lax.axis_index("epoch")
    my_j = lax.axis_index("space")
    me = my_i * n_space + my_j

    def epoch_peer(step):
        core = lax.rem(lax.rem(my_i, 2) + step % 2, 2)
        return lax.rem(my_i // 2 + step // 2, n_epoch // 2) * 2 + core

    def epoch_source(step):
        core = lax.rem(lax.rem(my_i, 2) + step % 2, 2)
        return lax.rem(my_i // 2 + n_epoch // 2 - step // 2, n_epoch // 2) * 2 + core

    steps = [
        (a, b)
        for b in reversed(range(n_space))
        for a in reversed(range(n_epoch))
        if a or b
    ]

    loading = pltpu.make_async_copy(x_hbm, x_ref, load)
    loading.start()
    barrier = pltpu.get_barrier_semaphore()
    for a, b in steps:
        pl.semaphore_signal(
            barrier,
            inc=1,
            device_id={"epoch": epoch_peer(a), "space": lax.rem(my_j + b, n_space)},
            device_id_type=MESH,
        )

    cut = (n_space * held * local, local * rows)
    at = iota(cut, 0)
    strip_of = over(at, held * local)
    row_of, own_of = rest(over(at, local), held), rest(at, local)
    pick_own, pick_row = over(iota(cut, 1), rows), rest(iota(cut, 1), rows)
    pick = one_hot((pick_own == own_of) & (pick_row == strip_of * strip + row_of - MARGIN))
    loading.wait()
    for k in range(2):
        picked = jnp.dot(pick, x_ref[k].reshape(local * rows, cols), preferred_element_type=F32)
        for i in range(n_epoch):
            piece = picked[:, i * width : (i + 1) * width]
            if lane_pad > width:
                piece = jnp.concatenate(
                    [piece, jnp.zeros((piece.shape[0], lane_pad - width), F32)], axis=1
                )
            piece = piece.astype(BF16)
            for j in range(n_space):
                strips[i * n_space + j, :, k * lane_pad : (k + 1) * lane_pad] = piece[
                    j * held * local : (j + 1) * held * local
                ]

    pl.semaphore_wait(barrier, len(steps))

    def first_copy(slot, to_i, to_j, source):
        return pltpu.make_async_remote_copy(
            src_ref=strips.at[to_i * n_space + to_j],
            dst_ref=parts.at[source],
            send_sem=send1.at[slot],
            recv_sem=recv1.at[source],
            device_id={"epoch": to_i, "space": to_j},
            device_id_type=MESH,
        )

    sent = []
    for slot, (a, b) in enumerate(steps):
        copy = first_copy(slot, epoch_peer(a), lax.rem(my_j + b, n_space), me)
        copy.start()
        sent.append(copy)
    parts[me] = strips[me]
    size = total * held
    to, fro = iota((size, size), 0), iota((size, size), 1)
    source_row = rest(over(fro, local), held)
    source_epoch = over(fro, held * local) * local + rest(fro, local)
    order[...] = one_hot((over(to, total) == source_row) & (rest(to, total) == source_epoch))
    look = rest(iota((lane_pad, lanes), 1), looks) * LOOKC
    col = iota((lane_pad, lanes), 0)
    fold[...] = jnp.where((col >= look) & (col < look + LOOKC), 1.0, 0.0)
    for slot, (a, b) in enumerate(steps):
        from_i, from_j = epoch_source(a), lax.rem(my_j + n_space - b, n_space)
        first_copy(slot, from_i, from_j, from_i * n_space + from_j).wait_recv()

    arrived = parts[...]
    if (held * local) % 16:
        arrived = arrived.astype(F32).reshape(size, 2 * lane_pad).astype(BF16)
    else:
        arrived = arrived.reshape(size, 2 * lane_pad)
    by_row = jnp.dot(order[...], arrived, preferred_element_type=F32)
    epochs[...] = by_row
    re, im = by_row[:, :lane_pad], by_row[:, lane_pad:]
    turned = jnp.concatenate([-im, re], axis=1).astype(BF16)
    plain = by_row.astype(BF16)
    for row in range(held):
        lefts[row, :total] = plain[row * total : (row + 1) * total]
        lefts[row, total:] = turned[row * total : (row + 1) * total]

    square = (re * re + im * im).reshape(held, total, lane_pad)
    summed = [
        functools.reduce(lambda p, q: p + q, [square[r + d] for d in range(LOOKR)])
        for r in range(strip)
    ]
    summed = jnp.concatenate(summed, axis=0)
    power = jnp.dot(summed, fold[...], preferred_element_type=F32, precision=lax.Precision.HIGHEST)
    power = power + 1e-06
    for r in range(strip):
        powers[r] = power[r * total : (r + 1) * total]

    window = iota((1, looks, 2 * lane_pad), 1) * LOOKC
    place = iota((1, looks, 2 * lane_pad), 2)
    place = jnp.where(place < lane_pad, place, place - lane_pad)
    inside = (place >= window) & (place < window + LOOKC)
    own_lane = over(iota((block, lanes), 1), looks) == iota((block, lanes), 0)

    def second_copy(slot, to_i, source):
        return pltpu.make_async_remote_copy(
            src_ref=coh.at[slot],
            dst_ref=got.at[source],
            send_sem=send2.at[slot],
            recv_sem=recv2.at[source],
            device_id={"epoch": to_i},
            device_id_type=MESH,
        )

    for step in reversed(range(n_epoch)):
        to_i = epoch_peer(step)
        first = to_i * block
        grams = []
        for row in range(held):
            start = row * total + first
            if block % 8 == 0:
                start = pl.multiple_of(start, 8)
            mine = epochs[pl.ds(start, block), :]
            masked = jnp.where(inside, mine[:, None, :], 0.0).astype(BF16)
            grams.append(
                lax.dot_general(
                    lefts[row],
                    masked.reshape(lanes, 2 * lane_pad),
                    (((1,), (1,)), ((), ())),
                    preferred_element_type=F32,
                )
            )
        for r in range(strip):
            cross = functools.reduce(lambda p, q: p + q, grams[r : r + LOOKR])
            left = powers[r, pl.ds(pl.multiple_of(first, 8) if block % 8 == 0 else first, block), :]
            left = jnp.sum(jnp.where(own_lane, left, 0.0), axis=0, keepdims=True)
            inverse = lax.rsqrt(left * powers[r])
            value = jnp.concatenate(
                [cross[:total] * inverse, cross[total:] * inverse], axis=0
            ).astype(BF16)
            if step:
                coh[step, r] = value
            else:
                got[my_i, r] = value
        if step:
            copy = second_copy(step, to_i, my_i)
            copy.start()
            sent.append(copy)

    for step in reversed(range(1, n_epoch)):
        from_i = epoch_source(step)
        second_copy(step, from_i, from_i).wait_recv()

    for copy in sent:
        copy.wait_send()


def spread_kernel(dims, got, out_hbm, out_ref, sem):
    n_epoch, block, total, strip, all_looks = dims
    looks = all_looks // n_epoch
    lanes = block * looks
    if lanes == LANES and (strip * n_epoch) % block == 0 and block & (block - 1) == 0:
        spot = over(iota((2 * total, lanes), 1), looks)
        copies = []
        for half in range(strip * n_epoch // block):
            tiles = []
            for t in range(half * block, (half + 1) * block):
                tiles.append(got[t % n_epoch, t // n_epoch].astype(F32))
            bit = 1
            while bit < block:
                low = spot & bit == 0
                turned_tiles = list(tiles)
                for t in range(block):
                    if t & bit:
                        continue
                    one, two = tiles[t], tiles[t + bit]
                    turned_tiles[t] = jnp.where(low, one, pltpu.roll(two, bit * looks, 1))
                    turned_tiles[t + bit] = jnp.where(
                        low, pltpu.roll(one, lanes - bit * looks, 1), two
                    )
                tiles = turned_tiles
                bit *= 2
            for e in range(block):
                value = tiles[e].astype(BF16)
                for k in range(2):
                    out_ref[k, e, :, half * lanes : (half + 1) * lanes] = value[
                        k * total : (k + 1) * total
                    ]
            side = pl.ds(half * lanes, lanes)
            copies.append(
                pltpu.make_async_copy(
                    out_ref.at[:, :, :, side], out_hbm.at[:, :, :, side], sem.at[half]
                )
            )
            copies[-1].start()
        for copy in copies:
            copy.wait()
    else:
        shape = (lanes, strip * all_looks)
        fro_e, fro_c, goal = iota(shape, 0) // looks, iota(shape, 0) % looks, iota(shape, 1)
        for e in range(block):

            def add(i, acc):
                for r in range(strip):
                    spread = one_hot((fro_e == e) & (goal == r * all_looks + i * looks + fro_c))
                    acc = acc + jnp.dot(got[i, r], spread, preferred_element_type=F32)
                return acc

            value = lax.fori_loop(0, n_epoch, add, jnp.zeros((2 * total, shape[1]), F32))
            value = value.astype(BF16)
            for k in range(2):
                out_ref[k, e] = value[k * total : (k + 1) * total]
        whole = pltpu.make_async_copy(out_ref, out_hbm, sem.at[0])
        whole.start()
        whole.wait()


def per_device(slc_stack):
    n_epoch, n_space = lax.axis_size("epoch"), lax.axis_size("space")
    _, local, rows, cols = slc_stack.shape
    strip = rows // n_space
    held = strip + 2 * MARGIN
    total = n_epoch * n_space * local
    block = n_space * local
    width = cols // n_epoch
    lane_pad = -(-width // LANES) * LANES
    lanes = block * (width // LOOKC)
    sources = n_epoch * n_space
    dims = (n_epoch, n_space, local, rows, cols, strip)
    all_looks = cols // LOOKC
    vmem = pl.BlockSpec(memory_space=pltpu.VMEM)
    hbm = pl.BlockSpec(memory_space=pl.ANY)
    got = pl.pallas_call(
        functools.partial(kernel, dims),
        out_shape=jax.ShapeDtypeStruct((n_epoch, strip, 2 * total, lanes), BF16),
        in_specs=[hbm],
        out_specs=vmem,
        scratch_shapes=[
            pltpu.VMEM(slc_stack.shape, BF16),
            pltpu.VMEM((sources, held * local, 2 * lane_pad), BF16),
            pltpu.VMEM((sources, held * local, 2 * lane_pad), BF16),
            pltpu.VMEM((held * total, 2 * lane_pad), F32),
            pltpu.VMEM((held, 2 * total, 2 * lane_pad), BF16),
            pltpu.VMEM((strip, total, lanes), F32),
            pltpu.VMEM((n_epoch, strip, 2 * total, lanes), BF16),
            pltpu.VMEM((held * total, held * total), BF16),
            pltpu.VMEM((lane_pad, lanes), F32),
            pltpu.SemaphoreType.DMA(()),
            pltpu.SemaphoreType.DMA((sources - 1,)),
            pltpu.SemaphoreType.DMA((sources,)),
            pltpu.SemaphoreType.DMA((n_epoch,)),
            pltpu.SemaphoreType.DMA((n_epoch,)),
        ],
        compiler_params=pltpu.CompilerParams(
            collective_id=0, has_side_effects=True, vmem_limit_bytes=48 * 1024 * 1024
        ),
        cost_estimate=pl.CostEstimate(flops=10**9, bytes_accessed=10**6, transcendentals=0),
    )(pltpu.with_memory_space_constraint(slc_stack, pltpu.HBM))
    out = jax.ShapeDtypeStruct((2, block, total, strip * all_looks), BF16)
    return pl.pallas_call(
        functools.partial(spread_kernel, (n_epoch, block, total, strip, all_looks)),
        out_shape=out,
        in_specs=[vmem],
        out_specs=hbm,
        scratch_shapes=[
            pltpu.VMEM(out.shape, BF16),
            pltpu.SemaphoreType.DMA((max(1, strip * n_epoch // block),)),
        ],
        compiler_params=pltpu.CompilerParams(vmem_limit_bytes=32 * 1024 * 1024),
    )(got)


def solution(mesh):
    in_specs = (P(None, ("epoch", "space"), "groups", None),)
    out_specs = P(None, "epoch", None, ("groups", "space"))
    return jax.shard_map(
        per_device, mesh=mesh, in_specs=in_specs, out_specs=out_specs, check_vma=False
    )
```

```python
import functools

import jax
import jax.numpy as jnp
from jax import lax
from jax.experimental import pallas as pl
from jax.experimental.pallas import tpu as pltpu
from jax.sharding import PartitionSpec as P

LOOKR = 5
LOOKC = 15
MARGIN = 2
LANES = 128
MESH = pl.DeviceIdType.MESH
F32 = jnp.float32
BF16 = jnp.bfloat16


def iota(shape, axis):
    return lax.broadcasted_iota(jnp.int32, shape, axis)


def one_hot(hits):
    return jnp.where(hits, 1.0, 0.0).astype(BF16)


def over(value, by):
    return value >> (by.bit_length() - 1) if by & (by - 1) == 0 else lax.div(value, by)


def rest(value, by):
    return value & (by - 1) if by & (by - 1) == 0 else lax.rem(value, by)


def kernel(dims, x_hbm, got, x_ref, cut, mid_out, edge_out, mid_in, edge_in, *rest_refs):
    n_epoch, n_space, local, rows, cols, strip, pieces, mid_rows, edge_rows = dims
    mid_order, edge_order, fold, lefts, epochs, folded, middle, coh = rest_refs[:8]
    load, send_mid, recv_mid, send_edge, recv_edge, send_coh, recv_coh = rest_refs[8:]
    total = n_epoch * n_space * local
    block = n_space * local
    held = strip + 2 * MARGIN
    width = cols // n_epoch
    part = width // pieces
    looks = width // LOOKC
    looks_part = looks // pieces
    planes = 2 * pieces
    lanes = block * looks
    my_i = lax.axis_index("epoch")
    my_j = lax.axis_index("space")
    me = my_i * n_space + my_j

    def epoch_peer(step):
        core = lax.rem(lax.rem(my_i, 2) + step % 2, 2)
        return lax.rem(my_i // 2 + step // 2, n_epoch // 2) * 2 + core

    def epoch_source(step):
        core = lax.rem(lax.rem(my_i, 2) + step % 2, 2)
        return lax.rem(my_i // 2 + n_epoch // 2 - step // 2, n_epoch // 2) * 2 + core

    steps = [
        (a, b)
        for b in reversed(range(n_space))
        for a in reversed(range(n_epoch))
        if a or b
    ]
    targets = [(epoch_peer(a), lax.rem(my_j + b, n_space)) for a, b in steps]
    origins = [(epoch_source(a), lax.rem(my_j + n_space - b, n_space)) for a, b in steps]

    loading = pltpu.make_async_copy(x_hbm, x_ref, load)
    loading.start()
    barrier = pltpu.get_barrier_semaphore()
    for to_i, to_j in targets:
        pl.semaphore_signal(
            barrier,
            inc=1,
            device_id={"epoch": to_i, "space": to_j},
            device_id_type=MESH,
        )

    def picker(count, size, sides, first):
        shape = (n_space * sides * size, planes * local * rows)
        goal, held_at = iota(shape, 0), iota(shape, 1)
        spot = rest(goal, size)
        row = over(spot, planes * local)
        wanted = over(goal, sides * size) * strip + row + first(rest(over(goal, size), sides))
        return one_hot(
            (row < count)
            & (rest(spot, planes) == over(held_at, local * rows))
            & (rest(over(spot, planes), local) == rest(over(held_at, rows), local))
            & (wanted == rest(held_at, rows))
        )

    pick = jnp.concatenate(
        [
            picker(strip, mid_rows, 1, lambda side: 0),
            picker(
                MARGIN, edge_rows, 2, lambda side: jnp.where(side == 0, -MARGIN, strip)
            ),
        ],
        axis=0,
    )
    loading.wait()
    for k in range(2):
        image = x_ref[k].reshape(local * rows, cols).astype(F32)
        for i in range(n_epoch):
            for h in range(pieces):
                start = i * width + h * part
                piece = image[:, start : start + part]
                if part < LANES:
                    blank = jnp.zeros((local * rows, LANES - part), F32)
                    piece = jnp.concatenate([piece, blank], axis=1)
                plane = k * pieces + h
                cut[
                    plane * local * rows : (plane + 1) * local * rows,
                    i * LANES : (i + 1) * LANES,
                ] = piece.astype(BF16)
    picked = jnp.dot(pick, cut[...], preferred_element_type=F32).astype(BF16)
    for i in range(n_epoch):
        side = slice(i * LANES, (i + 1) * LANES)
        for j in range(n_space):
            mid_out[i * n_space + j] = picked[j * mid_rows : (j + 1) * mid_rows, side]
            for z in range(2):
                start = n_space * mid_rows + (2 * j + z) * edge_rows
                edge_out[i * n_space + j, z] = picked[start : start + edge_rows, side]

    pl.semaphore_wait(barrier, len(steps))

    def mid_copy(slot, to_i, to_j, source):
        return pltpu.make_async_remote_copy(
            src_ref=mid_out.at[to_i * n_space + to_j],
            dst_ref=mid_in.at[source],
            send_sem=send_mid.at[slot],
            recv_sem=recv_mid.at[source],
            device_id={"epoch": to_i, "space": to_j},
            device_id_type=MESH,
        )

    def edge_copy(slot, to_i, to_j, source, low, count):
        return pltpu.make_async_remote_copy(
            src_ref=edge_out.at[to_i * n_space + to_j, pl.ds(low, count)],
            dst_ref=edge_in.at[source, pl.ds(low, count)],
            send_sem=send_edge.at[slot],
            recv_sem=recv_edge.at[source],
            device_id={"epoch": to_i, "space": to_j},
            device_id_type=MESH,
        )

    def by_place(j, act):
        if n_space > 1:
            pl.when(j == 0)(lambda: act(1, 1))
            pl.when(j == n_space - 1)(lambda: act(0, 1))
            pl.when((j > 0) & (j < n_space - 1))(lambda: act(0, 2))

    for slot, (to_i, to_j) in enumerate(targets):
        mid_copy(slot, to_i, to_j, me).start()
    for slot, (to_i, to_j) in enumerate(targets):
        by_place(
            to_j,
            lambda low, count: edge_copy(slot, to_i, to_j, me, low, count).start(),
        )

    @pl.when(my_j == 0)
    def _():
        edge_in[:, 0] = jnp.zeros((n_epoch * n_space, edge_rows, LANES), BF16)

    @pl.when(my_j == n_space - 1)
    def _():
        edge_in[:, 1] = jnp.zeros((n_epoch * n_space, edge_rows, LANES), BF16)

    mid_in[me] = mid_out[me]
    edge_in[me] = edge_out[me]

    def order(count, size):
        shape = (planes * count * total, n_epoch * n_space * size)
        goal, fro = iota(shape, 0), iota(shape, 1)
        spot = rest(fro, size)
        row = over(spot, planes * local)
        epoch = over(fro, size) * local + rest(over(spot, planes), local)
        want = (rest(spot, planes) * count + row) * total + epoch
        return one_hot((row < count) & (goal == want))

    mid_order[...] = order(strip, mid_rows)
    edge_order[...] = order(MARGIN, edge_rows)
    lane = iota((pieces * LANES, lanes), 0)
    look = rest(iota((pieces * LANES, lanes), 1), looks) - over(lane, LANES) * looks_part
    spare = rest(lane, LANES) - look * LOOKC
    fold[...] = jnp.where((spare >= 0) & (spare < LOOKC), 1.0, 0.0)
    lane = iota((1, looks, planes * LANES), 2)
    look = iota((1, looks, planes * LANES), 1) - rest(over(lane, LANES), pieces) * looks_part
    spare = rest(lane, LANES) - look * LOOKC
    inside = (spare >= 0) & (spare < LOOKC)
    own_lane = over(iota((block, lanes), 1), looks) == iota((block, lanes), 0)

    def settle(order_ref, arrived, held_rows):
        count = len(held_rows)
        sorted_rows = jnp.dot(order_ref[...], arrived, preferred_element_type=F32)
        size = count * total
        whole = [sorted_rows[p * size : (p + 1) * size] for p in range(planes)]
        re = jnp.concatenate(whole[:pieces], axis=1)
        im = jnp.concatenate(whole[pieces:], axis=1)
        plain = jnp.concatenate([re, im], axis=1)
        turned = jnp.concatenate([-im, re], axis=1).astype(BF16)
        packed = plain.astype(BF16)
        sums = jnp.dot(
            re * re + im * im,
            fold[...],
            preferred_element_type=F32,
            precision=lax.Precision.HIGHEST,
        )
        for n, row in enumerate(held_rows):
            part_of = slice(n * total, (n + 1) * total)
            epochs[row] = plain[part_of]
            lefts[row, :total] = packed[part_of]
            lefts[row, total:] = turned[part_of]
            folded[row] = sums[part_of]

    def place_of(group):
        first = group * block
        return pl.ds(pl.multiple_of(first, 8) if block % 8 == 0 else first, block)

    def gram(row, group):
        masked = jnp.where(inside, epochs[row, place_of(group), :][:, None, :], 0.0)
        return lax.dot_general(
            lefts[row],
            masked.astype(BF16).reshape(lanes, planes * LANES),
            (((1,), (1,)), ((), ())),
            preferred_element_type=F32,
        )

    def add_up(terms):
        return functools.reduce(lambda p, q: p + q, terms)

    own_rows = list(range(MARGIN, MARGIN + strip))
    edge_sides = [list(range(MARGIN)), list(range(MARGIN + strip, held))]
    windows = [range(r, r + LOOKR) for r in range(strip)]

    for slot, (from_i, from_j) in enumerate(origins):
        mid_copy(slot, from_i, from_j, from_i * n_space + from_j).wait_recv()
    settle(mid_order, mid_in[...].reshape(n_epoch * n_space * mid_rows, LANES), own_rows)
    for group in range(n_epoch):
        grams = {row: gram(row, group) for row in own_rows}
        for r in range(strip):
            middle[group, r] = add_up([grams[row] for row in windows[r] if row in grams])

    for slot, (from_i, from_j) in enumerate(origins):
        by_place(
            my_j,
            lambda low, count: edge_copy(
                slot, from_i, from_j, from_i * n_space + from_j, low, count
            ).wait_recv(),
        )
    for z in range(2):
        arrived = edge_in[:, z].reshape(n_epoch * n_space * edge_rows, LANES)
        settle(edge_order, arrived, edge_sides[z])

    def coh_copy(slot, to_i, source):
        return pltpu.make_async_remote_copy(
            src_ref=coh.at[slot],
            dst_ref=got.at[source],
            send_sem=send_coh.at[slot],
            recv_sem=recv_coh.at[source],
            device_id={"epoch": to_i},
            device_id_type=MESH,
        )

    for step in reversed(range(n_epoch)):
        to_i = epoch_peer(step)
        grams = {row: gram(row, to_i) for rows_of in edge_sides for row in rows_of}
        for r in range(strip):
            cross = middle[to_i, r] + add_up([grams[row] for row in windows[r] if row in grams])
            power = add_up([folded[row] for row in windows[r]]) + 1e-06
            left = add_up([folded[row, place_of(to_i), :] for row in windows[r]]) + 1e-06
            left = jnp.sum(jnp.where(own_lane, left, 0.0), axis=0, keepdims=True)
            inverse = lax.rsqrt(left * power)
            value = jnp.concatenate(
                [cross[:total] * inverse, cross[total:] * inverse], axis=0
            ).astype(BF16)
            if step:
                coh[step, r] = value
            else:
                got[my_i, r] = value
        if step:
            coh_copy(step, to_i, my_i).start()

    for step in reversed(range(1, n_epoch)):
        from_i = epoch_source(step)
        coh_copy(step, from_i, from_i).wait_recv()
    for step in range(1, n_epoch):
        coh_copy(step, epoch_peer(step), my_i).wait_send()
    for slot, (to_i, to_j) in enumerate(targets):
        mid_copy(slot, to_i, to_j, me).wait_send()
        by_place(
            to_j,
            lambda low, count: edge_copy(slot, to_i, to_j, me, low, count).wait_send(),
        )


def spread_kernel(dims, got, out_hbm, out_ref, sem):
    n_epoch, block, total, strip, all_looks = dims
    looks = all_looks // n_epoch
    lanes = block * looks
    if lanes == LANES and (strip * n_epoch) % block == 0 and block & (block - 1) == 0:
        spot = over(iota((2 * total, lanes), 1), looks)
        copies = []
        for half in range(strip * n_epoch // block):
            tiles = []
            for t in range(half * block, (half + 1) * block):
                tiles.append(got[t % n_epoch, t // n_epoch].astype(F32))
            bit = 1
            while bit < block:
                low = spot & bit == 0
                turned_tiles = list(tiles)
                for t in range(block):
                    if t & bit:
                        continue
                    one, two = tiles[t], tiles[t + bit]
                    turned_tiles[t] = jnp.where(low, one, pltpu.roll(two, bit * looks, 1))
                    turned_tiles[t + bit] = jnp.where(
                        low, pltpu.roll(one, lanes - bit * looks, 1), two
                    )
                tiles = turned_tiles
                bit *= 2
            for e in range(block):
                value = tiles[e].astype(BF16)
                for k in range(2):
                    out_ref[k, e, :, half * lanes : (half + 1) * lanes] = value[
                        k * total : (k + 1) * total
                    ]
            side = pl.ds(half * lanes, lanes)
            copies.append(
                pltpu.make_async_copy(
                    out_ref.at[:, :, :, side], out_hbm.at[:, :, :, side], sem.at[half]
                )
            )
            copies[-1].start()
        for copy in copies:
            copy.wait()
    else:
        shape = (lanes, strip * all_looks)
        fro_e, fro_c, goal = iota(shape, 0) // looks, iota(shape, 0) % looks, iota(shape, 1)
        for e in range(block):

            def add(i, acc):
                for r in range(strip):
                    spread = one_hot((fro_e == e) & (goal == r * all_looks + i * looks + fro_c))
                    acc = acc + jnp.dot(got[i, r], spread, preferred_element_type=F32)
                return acc

            value = lax.fori_loop(0, n_epoch, add, jnp.zeros((2 * total, shape[1]), F32))
            value = value.astype(BF16)
            for k in range(2):
                out_ref[k, e] = value[k * total : (k + 1) * total]
        whole = pltpu.make_async_copy(out_ref, out_hbm, sem.at[0])
        whole.start()
        whole.wait()


def per_device(slc_stack):
    n_epoch, n_space = lax.axis_size("epoch"), lax.axis_size("space")
    _, local, rows, cols = slc_stack.shape
    strip = rows // n_space
    held = strip + 2 * MARGIN
    total = n_epoch * n_space * local
    block = n_space * local
    width = cols // n_epoch
    looks = width // LOOKC
    all_looks = cols // LOOKC
    lanes = block * looks
    pieces = next(p for p in range(1, looks + 1) if looks % p == 0 and width // p <= LANES)
    planes = 2 * pieces
    mid_rows = -(-strip * local * planes // 16) * 16
    edge_rows = -(-MARGIN * local * planes // 16) * 16
    sources = n_epoch * n_space
    dims = (n_epoch, n_space, local, rows, cols, strip, pieces, mid_rows, edge_rows)
    vmem = pl.BlockSpec(memory_space=pltpu.VMEM)
    hbm = pl.BlockSpec(memory_space=pl.ANY)
    got = pl.pallas_call(
        functools.partial(kernel, dims),
        out_shape=jax.ShapeDtypeStruct((n_epoch, strip, 2 * total, lanes), BF16),
        in_specs=[hbm],
        out_specs=vmem,
        scratch_shapes=[
            pltpu.VMEM(slc_stack.shape, BF16),
            pltpu.VMEM((planes * local * rows, n_epoch * LANES), BF16),
            pltpu.VMEM((sources, mid_rows, LANES), BF16),
            pltpu.VMEM((sources, 2, edge_rows, LANES), BF16),
            pltpu.VMEM((sources, mid_rows, LANES), BF16),
            pltpu.VMEM((sources, 2, edge_rows, LANES), BF16),
            pltpu.VMEM((planes * strip * total, sources * mid_rows), BF16),
            pltpu.VMEM((planes * MARGIN * total, sources * edge_rows), BF16),
            pltpu.VMEM((pieces * LANES, lanes), F32),
            pltpu.VMEM((held, 2 * total, planes * LANES), BF16),
            pltpu.VMEM((held, total, planes * LANES), F32),
            pltpu.VMEM((held, total, lanes), F32),
            pltpu.VMEM((n_epoch, strip, 2 * total, lanes), F32),
            pltpu.VMEM((n_epoch, strip, 2 * total, lanes), BF16),
            pltpu.SemaphoreType.DMA(()),
            pltpu.SemaphoreType.DMA((sources - 1,)),
            pltpu.SemaphoreType.DMA((sources,)),
            pltpu.SemaphoreType.DMA((sources - 1,)),
            pltpu.SemaphoreType.DMA((sources,)),
            pltpu.SemaphoreType.DMA((n_epoch,)),
            pltpu.SemaphoreType.DMA((n_epoch,)),
        ],
        compiler_params=pltpu.CompilerParams(
            collective_id=0, has_side_effects=True, vmem_limit_bytes=48 * 1024 * 1024
        ),
        cost_estimate=pl.CostEstimate(flops=10**9, bytes_accessed=10**6, transcendentals=0),
    )(pltpu.with_memory_space_constraint(slc_stack, pltpu.HBM))
    out = jax.ShapeDtypeStruct((2, block, total, strip * all_looks), BF16)
    return pl.pallas_call(
        functools.partial(spread_kernel, (n_epoch, block, total, strip, all_looks)),
        out_shape=out,
        in_specs=[vmem],
        out_specs=hbm,
        scratch_shapes=[
            pltpu.VMEM(out.shape, BF16),
            pltpu.SemaphoreType.DMA((max(1, strip * n_epoch // block),)),
        ],
        compiler_params=pltpu.CompilerParams(vmem_limit_bytes=32 * 1024 * 1024),
    )(got)


def solution(mesh):
    in_specs = (P(None, ("epoch", "space"), "groups", None),)
    out_specs = P(None, "epoch", None, ("groups", "space"))
    return jax.shard_map(
        per_device, mesh=mesh, in_specs=in_specs, out_specs=out_specs, check_vma=False
    )
```

```python
import functools

import jax
import jax.numpy as jnp
from jax import lax
from jax.experimental import pallas as pl
from jax.experimental.pallas import tpu as pltpu
from jax.sharding import PartitionSpec as P

LOOKR = 5
LOOKC = 15
MARGIN = 2
LANES = 128
MESH = pl.DeviceIdType.MESH
F32 = jnp.float32
BF16 = jnp.bfloat16


def iota(shape, axis):
    return lax.broadcasted_iota(jnp.int32, shape, axis)


def one_hot(hits):
    return jnp.where(hits, 1.0, 0.0).astype(BF16)


def over(value, by):
    return value >> (by.bit_length() - 1) if by & (by - 1) == 0 else lax.div(value, by)


def rest(value, by):
    return value & (by - 1) if by & (by - 1) == 0 else lax.rem(value, by)


def kernel(dims, x_hbm, got, x_ref, cut, mid_out, edge_out, mid_in, edge_in, *rest_refs):
    n_epoch, n_space, local, rows, cols, strip, pieces, mid_rows, edge_rows = dims
    mid_order, edge_order, fold, lefts, epochs, folded, middle, coh = rest_refs[:8]
    load, send_mid, recv_mid, send_edge, recv_edge, send_coh, recv_coh = rest_refs[8:]
    total = n_epoch * n_space * local
    block = n_space * local
    held = strip + 2 * MARGIN
    width = cols // n_epoch
    part = width // pieces
    looks = width // LOOKC
    looks_part = looks // pieces
    planes = 2 * pieces
    lanes = block * looks
    my_i = lax.axis_index("epoch")
    my_j = lax.axis_index("space")
    me = my_i * n_space + my_j

    def epoch_peer(step):
        core = lax.rem(lax.rem(my_i, 2) + step % 2, 2)
        return lax.rem(my_i // 2 + step // 2, n_epoch // 2) * 2 + core

    def epoch_source(step):
        core = lax.rem(lax.rem(my_i, 2) + step % 2, 2)
        return lax.rem(my_i // 2 + n_epoch // 2 - step // 2, n_epoch // 2) * 2 + core

    steps = [
        (a, b)
        for b in reversed(range(n_space))
        for a in reversed(range(n_epoch))
        if a or b
    ]
    targets = [(epoch_peer(a), lax.rem(my_j + b, n_space)) for a, b in steps]
    origins = [(epoch_source(a), lax.rem(my_j + n_space - b, n_space)) for a, b in steps]

    loading = pltpu.make_async_copy(x_hbm, x_ref, load)
    loading.start()
    barrier = pltpu.get_barrier_semaphore()
    for to_i, to_j in targets:
        pl.semaphore_signal(
            barrier,
            inc=1,
            device_id={"epoch": to_i, "space": to_j},
            device_id_type=MESH,
        )

    def picker(count, size, sides, first):
        shape = (n_space * sides * size, planes * local * rows)
        goal, held_at = iota(shape, 0), iota(shape, 1)
        spot = rest(goal, size)
        row = over(spot, planes * local)
        wanted = over(goal, sides * size) * strip + row + first(rest(over(goal, size), sides))
        return one_hot(
            (row < count)
            & (rest(spot, planes) == over(held_at, local * rows))
            & (rest(over(spot, planes), local) == rest(over(held_at, rows), local))
            & (wanted == rest(held_at, rows))
        )

    pick = jnp.concatenate(
        [
            picker(strip, mid_rows, 1, lambda side: 0),
            picker(
                MARGIN, edge_rows, 2, lambda side: jnp.where(side == 0, -MARGIN, strip)
            ),
        ],
        axis=0,
    )
    loading.wait()
    for k in range(2):
        image = x_ref[k].reshape(local * rows, cols).astype(F32)
        for i in range(n_epoch):
            for h in range(pieces):
                start = i * width + h * part
                piece = image[:, start : start + part]
                if part < LANES:
                    blank = jnp.zeros((local * rows, LANES - part), F32)
                    piece = jnp.concatenate([piece, blank], axis=1)
                plane = k * pieces + h
                cut[
                    plane * local * rows : (plane + 1) * local * rows,
                    i * LANES : (i + 1) * LANES,
                ] = piece.astype(BF16)
    picked = jnp.dot(pick, cut[...], preferred_element_type=F32).astype(BF16)
    for i in range(n_epoch):
        side = slice(i * LANES, (i + 1) * LANES)
        for j in range(n_space):
            mid_out[i * n_space + j] = picked[j * mid_rows : (j + 1) * mid_rows, side]
            for z in range(2):
                start = n_space * mid_rows + (2 * j + z) * edge_rows
                edge_out[i * n_space + j, z] = picked[start : start + edge_rows, side]

    pl.semaphore_wait(barrier, len(steps))

    def mid_copy(slot, to_i, to_j, source):
        return pltpu.make_async_remote_copy(
            src_ref=mid_out.at[to_i * n_space + to_j],
            dst_ref=mid_in.at[source],
            send_sem=send_mid.at[slot],
            recv_sem=recv_mid.at[source],
            device_id={"epoch": to_i, "space": to_j},
            device_id_type=MESH,
        )

    def edge_copy(slot, to_i, to_j, source, low, count):
        return pltpu.make_async_remote_copy(
            src_ref=edge_out.at[to_i * n_space + to_j, pl.ds(low, count)],
            dst_ref=edge_in.at[source, pl.ds(low, count)],
            send_sem=send_edge.at[slot],
            recv_sem=recv_edge.at[source],
            device_id={"epoch": to_i, "space": to_j},
            device_id_type=MESH,
        )

    def by_place(j, act):
        if n_space > 1:
            pl.when(j == 0)(lambda: act(1, 1))
            pl.when(j == n_space - 1)(lambda: act(0, 1))
            pl.when((j > 0) & (j < n_space - 1))(lambda: act(0, 2))

    for slot, (to_i, to_j) in enumerate(targets):
        mid_copy(slot, to_i, to_j, me).start()
    for slot, (to_i, to_j) in enumerate(targets):
        by_place(
            to_j,
            lambda low, count: edge_copy(slot, to_i, to_j, me, low, count).start(),
        )

    @pl.when(my_j == 0)
    def _():
        edge_in[:, 0] = jnp.zeros((n_epoch * n_space, edge_rows, LANES), BF16)

    @pl.when(my_j == n_space - 1)
    def _():
        edge_in[:, 1] = jnp.zeros((n_epoch * n_space, edge_rows, LANES), BF16)

    mid_in[me] = mid_out[me]
    edge_in[me] = edge_out[me]

    def order(count, size):
        shape = (planes * count * total, n_epoch * n_space * size)
        goal, fro = iota(shape, 0), iota(shape, 1)
        spot = rest(fro, size)
        row = over(spot, planes * local)
        epoch = over(fro, size) * local + rest(over(spot, planes), local)
        want = (rest(spot, planes) * count + row) * total + epoch
        return one_hot((row < count) & (goal == want))

    mid_order[...] = order(strip, mid_rows)
    edge_order[...] = order(MARGIN, edge_rows)
    lane = iota((pieces * LANES, lanes), 0)
    look = rest(iota((pieces * LANES, lanes), 1), looks) - over(lane, LANES) * looks_part
    spare = rest(lane, LANES) - look * LOOKC
    fold[...] = jnp.where((spare >= 0) & (spare < LOOKC), 1.0, 0.0)
    lane = iota((1, looks, planes * LANES), 2)
    look = iota((1, looks, planes * LANES), 1) - rest(over(lane, LANES), pieces) * looks_part
    spare = rest(lane, LANES) - look * LOOKC
    inside = (spare >= 0) & (spare < LOOKC)
    own_lane = over(iota((block, lanes), 1), looks) == iota((block, lanes), 0)

    def settle(order_ref, arrived, held_rows):
        count = len(held_rows)
        sorted_rows = jnp.dot(order_ref[...], arrived, preferred_element_type=F32)
        size = count * total
        whole = [sorted_rows[p * size : (p + 1) * size] for p in range(planes)]
        re = jnp.concatenate(whole[:pieces], axis=1)
        im = jnp.concatenate(whole[pieces:], axis=1)
        plain = jnp.concatenate([re, im], axis=1)
        turned = jnp.concatenate([-im, re], axis=1)
        sums = jnp.dot(
            re * re + im * im,
            fold[...],
            preferred_element_type=F32,
            precision=lax.Precision.HIGHEST,
        )
        for n, row in enumerate(held_rows):
            part_of = slice(n * total, (n + 1) * total)
            epochs[row] = plain[part_of]
            factor = jnp.concatenate([plain[part_of], turned[part_of]], axis=0)
            lefts[row] = factor.T.astype(BF16)
            folded[row] = sums[part_of]

    def place_of(group):
        first = group * block
        return pl.ds(pl.multiple_of(first, 8) if block % 8 == 0 else first, block)

    def gram(row, images):
        masked = jnp.where(inside, images[:, None, :], 0.0).astype(BF16)
        masked = masked.reshape(images.shape[0] * looks, planes * LANES)
        return jnp.dot(masked, lefts[row], preferred_element_type=F32)

    def add_up(terms):
        return functools.reduce(lambda p, q: p + q, terms)

    own_rows = list(range(MARGIN, MARGIN + strip))
    edge_sides = [list(range(MARGIN)), list(range(MARGIN + strip, held))]
    windows = [range(r, r + LOOKR) for r in range(strip)]

    for slot, (from_i, from_j) in enumerate(origins):
        mid_copy(slot, from_i, from_j, from_i * n_space + from_j).wait_recv()
    settle(mid_order, mid_in[...].reshape(n_epoch * n_space * mid_rows, LANES), own_rows)
    for group in range(n_epoch):
        share = slice(group * block, (group + 1) * block)
        grams = {row: gram(row, epochs[row, share, :]) for row in own_rows}
        for r in range(strip):
            middle[group, r] = add_up([grams[row] for row in windows[r] if row in grams])

    for slot, (from_i, from_j) in enumerate(origins):
        by_place(
            my_j,
            lambda low, count: edge_copy(
                slot, from_i, from_j, from_i * n_space + from_j, low, count
            ).wait_recv(),
        )
    for z in range(2):
        arrived = edge_in[:, z].reshape(n_epoch * n_space * edge_rows, LANES)
        settle(edge_order, arrived, edge_sides[z])

    def coh_copy(slot, to_i, source):
        return pltpu.make_async_remote_copy(
            src_ref=coh.at[slot],
            dst_ref=got.at[source],
            send_sem=send_coh.at[slot],
            recv_sem=recv_coh.at[source],
            device_id={"epoch": to_i},
            device_id_type=MESH,
        )

    for step in reversed(range(n_epoch)):
        to_i = epoch_peer(step)
        grams = {
            row: gram(row, epochs[row, place_of(to_i), :])
            for rows_of in edge_sides
            for row in rows_of
        }
        for r in range(strip):
            cross = middle[to_i, r] + add_up([grams[row] for row in windows[r] if row in grams])
            cross = cross.T
            power = add_up([folded[row] for row in windows[r]]) + 1e-06
            left = add_up([folded[row, place_of(to_i), :] for row in windows[r]]) + 1e-06
            left = jnp.sum(jnp.where(own_lane, left, 0.0), axis=0, keepdims=True)
            inverse = lax.rsqrt(left * power)
            value = jnp.concatenate(
                [cross[:total] * inverse, cross[total:] * inverse], axis=0
            ).astype(BF16)
            if step:
                coh[step, r] = value
            else:
                got[my_i, r] = value
        if step:
            coh_copy(step, to_i, my_i).start()

    for step in reversed(range(1, n_epoch)):
        from_i = epoch_source(step)
        coh_copy(step, from_i, from_i).wait_recv()
    for step in range(1, n_epoch):
        coh_copy(step, epoch_peer(step), my_i).wait_send()
    for slot, (to_i, to_j) in enumerate(targets):
        mid_copy(slot, to_i, to_j, me).wait_send()
        by_place(
            to_j,
            lambda low, count: edge_copy(slot, to_i, to_j, me, low, count).wait_send(),
        )


def spread_kernel(dims, got, out_hbm, out_ref, sem):
    n_epoch, block, total, strip, all_looks = dims
    looks = all_looks // n_epoch
    lanes = block * looks
    if lanes == LANES and (strip * n_epoch) % block == 0 and block & (block - 1) == 0:
        spot = over(iota((2 * total, lanes), 1), looks)
        copies = []
        for half in range(strip * n_epoch // block):
            tiles = []
            for t in range(half * block, (half + 1) * block):
                tiles.append(got[t % n_epoch, t // n_epoch].astype(F32))
            bit = 1
            while bit < block:
                low = spot & bit == 0
                turned_tiles = list(tiles)
                for t in range(block):
                    if t & bit:
                        continue
                    one, two = tiles[t], tiles[t + bit]
                    turned_tiles[t] = jnp.where(low, one, pltpu.roll(two, bit * looks, 1))
                    turned_tiles[t + bit] = jnp.where(
                        low, pltpu.roll(one, lanes - bit * looks, 1), two
                    )
                tiles = turned_tiles
                bit *= 2
            for e in range(block):
                value = tiles[e].astype(BF16)
                for k in range(2):
                    out_ref[k, e, :, half * lanes : (half + 1) * lanes] = value[
                        k * total : (k + 1) * total
                    ]
            side = pl.ds(half * lanes, lanes)
            copies.append(
                pltpu.make_async_copy(
                    out_ref.at[:, :, :, side], out_hbm.at[:, :, :, side], sem.at[half]
                )
            )
            copies[-1].start()
        for copy in copies:
            copy.wait()
    else:
        shape = (lanes, strip * all_looks)
        fro_e, fro_c, goal = iota(shape, 0) // looks, iota(shape, 0) % looks, iota(shape, 1)
        for e in range(block):

            def add(i, acc):
                for r in range(strip):
                    spread = one_hot((fro_e == e) & (goal == r * all_looks + i * looks + fro_c))
                    acc = acc + jnp.dot(got[i, r], spread, preferred_element_type=F32)
                return acc

            value = lax.fori_loop(0, n_epoch, add, jnp.zeros((2 * total, shape[1]), F32))
            value = value.astype(BF16)
            for k in range(2):
                out_ref[k, e] = value[k * total : (k + 1) * total]
        whole = pltpu.make_async_copy(out_ref, out_hbm, sem.at[0])
        whole.start()
        whole.wait()


def per_device(slc_stack):
    n_epoch, n_space = lax.axis_size("epoch"), lax.axis_size("space")
    _, local, rows, cols = slc_stack.shape
    strip = rows // n_space
    held = strip + 2 * MARGIN
    total = n_epoch * n_space * local
    block = n_space * local
    width = cols // n_epoch
    looks = width // LOOKC
    all_looks = cols // LOOKC
    lanes = block * looks
    pieces = next(p for p in range(1, looks + 1) if looks % p == 0 and width // p <= LANES)
    planes = 2 * pieces
    mid_rows = -(-strip * local * planes // 16) * 16
    edge_rows = -(-MARGIN * local * planes // 16) * 16
    sources = n_epoch * n_space
    dims = (n_epoch, n_space, local, rows, cols, strip, pieces, mid_rows, edge_rows)
    vmem = pl.BlockSpec(memory_space=pltpu.VMEM)
    hbm = pl.BlockSpec(memory_space=pl.ANY)
    got = pl.pallas_call(
        functools.partial(kernel, dims),
        out_shape=jax.ShapeDtypeStruct((n_epoch, strip, 2 * total, lanes), BF16),
        in_specs=[hbm],
        out_specs=vmem,
        scratch_shapes=[
            pltpu.VMEM(slc_stack.shape, BF16),
            pltpu.VMEM((planes * local * rows, n_epoch * LANES), BF16),
            pltpu.VMEM((sources, mid_rows, LANES), BF16),
            pltpu.VMEM((sources, 2, edge_rows, LANES), BF16),
            pltpu.VMEM((sources, mid_rows, LANES), BF16),
            pltpu.VMEM((sources, 2, edge_rows, LANES), BF16),
            pltpu.VMEM((planes * strip * total, sources * mid_rows), BF16),
            pltpu.VMEM((planes * MARGIN * total, sources * edge_rows), BF16),
            pltpu.VMEM((pieces * LANES, lanes), F32),
            pltpu.VMEM((held, planes * LANES, 2 * total), BF16),
            pltpu.VMEM((held, total, planes * LANES), F32),
            pltpu.VMEM((held, total, lanes), F32),
            pltpu.VMEM((n_epoch, strip, lanes, 2 * total), F32),
            pltpu.VMEM((n_epoch, strip, 2 * total, lanes), BF16),
            pltpu.SemaphoreType.DMA(()),
            pltpu.SemaphoreType.DMA((sources - 1,)),
            pltpu.SemaphoreType.DMA((sources,)),
            pltpu.SemaphoreType.DMA((sources - 1,)),
            pltpu.SemaphoreType.DMA((sources,)),
            pltpu.SemaphoreType.DMA((n_epoch,)),
            pltpu.SemaphoreType.DMA((n_epoch,)),
        ],
        compiler_params=pltpu.CompilerParams(
            collective_id=0, has_side_effects=True, vmem_limit_bytes=48 * 1024 * 1024
        ),
        cost_estimate=pl.CostEstimate(flops=10**9, bytes_accessed=10**6, transcendentals=0),
    )(pltpu.with_memory_space_constraint(slc_stack, pltpu.HBM))
    out = jax.ShapeDtypeStruct((2, block, total, strip * all_looks), BF16)
    return pl.pallas_call(
        functools.partial(spread_kernel, (n_epoch, block, total, strip, all_looks)),
        out_shape=out,
        in_specs=[vmem],
        out_specs=hbm,
        scratch_shapes=[
            pltpu.VMEM(out.shape, BF16),
            pltpu.SemaphoreType.DMA((max(1, strip * n_epoch // block),)),
        ],
        compiler_params=pltpu.CompilerParams(vmem_limit_bytes=32 * 1024 * 1024),
    )(got)


def solution(mesh):
    in_specs = (P(None, ("epoch", "space"), "groups", None),)
    out_specs = P(None, "epoch", None, ("groups", "space"))
    return jax.shard_map(
        per_device, mesh=mesh, in_specs=in_specs, out_specs=out_specs, check_vma=False
    )
```

```python
import functools

import jax
import jax.numpy as jnp
from jax import lax
from jax.experimental import pallas as pl
from jax.experimental.pallas import tpu as pltpu
from jax.sharding import PartitionSpec as P

LOOKR = 5
LOOKC = 15
MARGIN = 2
LANES = 128
MESH = pl.DeviceIdType.MESH
F32 = jnp.float32
BF16 = jnp.bfloat16


def iota(shape, axis):
    return lax.broadcasted_iota(jnp.int32, shape, axis)


def one_hot(hits):
    return jnp.where(hits, 1.0, 0.0).astype(BF16)


def over(value, by):
    return value >> (by.bit_length() - 1) if by & (by - 1) == 0 else lax.div(value, by)


def rest(value, by):
    return value & (by - 1) if by & (by - 1) == 0 else lax.rem(value, by)


def kernel(dims, x_hbm, got, x_ref, cut, strips, parts, *rest_refs):
    n_epoch, n_space, local, rows, cols, strip, pieces, size = dims
    order, fold, lefts, epochs, folded, middle, coh = rest_refs[:7]
    load, send_strip, recv_strip, send_coh, recv_coh = rest_refs[7:]
    total = n_epoch * n_space * local
    block = n_space * local
    held = strip + 2 * MARGIN
    chunks = held // MARGIN
    width = cols // n_epoch
    part = width // pieces
    looks = width // LOOKC
    looks_part = looks // pieces
    planes = 2 * pieces
    lanes = block * looks
    my_i = lax.axis_index("epoch")
    my_j = lax.axis_index("space")
    me = my_i * n_space + my_j

    def epoch_peer(step):
        core = lax.rem(lax.rem(my_i, 2) + step % 2, 2)
        return lax.rem(my_i // 2 + step // 2, n_epoch // 2) * 2 + core

    def epoch_source(step):
        core = lax.rem(lax.rem(my_i, 2) + step % 2, 2)
        return lax.rem(my_i // 2 + n_epoch // 2 - step // 2, n_epoch // 2) * 2 + core

    steps = [
        (a, b)
        for b in reversed(range(n_space))
        for a in reversed(range(n_epoch))
        if a or b
    ]
    targets = [(epoch_peer(a), lax.rem(my_j + b, n_space)) for a, b in steps]
    origins = [(epoch_source(a), lax.rem(my_j + n_space - b, n_space)) for a, b in steps]

    loading = pltpu.make_async_copy(x_hbm, x_ref, load)
    loading.start()
    barrier = pltpu.get_barrier_semaphore()
    for to_i, to_j in targets:
        pl.semaphore_signal(
            barrier,
            inc=1,
            device_id={"epoch": to_i, "space": to_j},
            device_id_type=MESH,
        )

    shape = (n_space * chunks * size, planes * local * rows)
    goal, held_at = iota(shape, 0), iota(shape, 1)
    spot = rest(goal, size)
    row = over(spot, planes * local)
    first = over(goal, chunks * size) * strip - MARGIN
    wanted = first + rest(over(goal, size), chunks) * MARGIN + row
    pick = one_hot(
        (row < MARGIN)
        & (rest(spot, planes) == over(held_at, local * rows))
        & (rest(over(spot, planes), local) == rest(over(held_at, rows), local))
        & (wanted == rest(held_at, rows))
    )
    loading.wait()
    for k in range(2):
        image = x_ref[k].reshape(local * rows, cols).astype(F32)
        for i in range(n_epoch):
            for h in range(pieces):
                start = i * width + h * part
                piece = image[:, start : start + part]
                if part < LANES:
                    blank = jnp.zeros((local * rows, LANES - part), F32)
                    piece = jnp.concatenate([piece, blank], axis=1)
                plane = k * pieces + h
                cut[
                    plane * local * rows : (plane + 1) * local * rows,
                    i * LANES : (i + 1) * LANES,
                ] = piece.astype(BF16)
    picked = jnp.dot(pick, cut[...], preferred_element_type=F32).astype(BF16)
    for i in range(n_epoch):
        side = slice(i * LANES, (i + 1) * LANES)
        for j in range(n_space):
            for z in range(chunks):
                start = (j * chunks + z) * size
                strips[i * n_space + j, z] = picked[start : start + size, side]

    pl.semaphore_wait(barrier, len(steps))

    def strip_copy(part, slot, to_i, to_j, source, low, count):
        return pltpu.make_async_remote_copy(
            src_ref=strips.at[to_i * n_space + to_j, pl.ds(low, count)],
            dst_ref=parts.at[source, pl.ds(low, count)],
            send_sem=send_strip.at[part, slot],
            recv_sem=recv_strip.at[part, source],
            device_id={"epoch": to_i, "space": to_j},
            device_id_type=MESH,
        )

    def by_place(part, j, act):
        if part == 0:
            pl.when(j == 0)(lambda: act(1, chunks - 2))
            pl.when(j > 0)(lambda: act(0, chunks - 1))
        else:
            pl.when(j < n_space - 1)(lambda: act(chunks - 1, 1))

    for part_of in range(2):
        for slot, (to_i, to_j) in enumerate(targets):
            by_place(
                part_of,
                to_j,
                lambda low, count: strip_copy(
                    part_of, slot, to_i, to_j, me, low, count
                ).start(),
            )

    @pl.when(my_j == 0)
    def _():
        parts[:, 0] = jnp.zeros((n_epoch * n_space, size, LANES), BF16)

    @pl.when(my_j == n_space - 1)
    def _():
        parts[:, chunks - 1] = jnp.zeros((n_epoch * n_space, size, LANES), BF16)

    parts[me] = strips[me]

    shape = (planes * MARGIN * total, n_epoch * n_space * size)
    goal, fro = iota(shape, 0), iota(shape, 1)
    spot = rest(fro, size)
    row = over(spot, planes * local)
    epoch = over(fro, size) * local + rest(over(spot, planes), local)
    want = (rest(spot, planes) * MARGIN + row) * total + epoch
    order[...] = one_hot((row < MARGIN) & (goal == want))
    lane = iota((pieces * LANES, lanes), 0)
    look = rest(iota((pieces * LANES, lanes), 1), looks) - over(lane, LANES) * looks_part
    spare = rest(lane, LANES) - look * LOOKC
    fold[...] = jnp.where((spare >= 0) & (spare < LOOKC), 1.0, 0.0)
    lane = iota((1, looks, planes * LANES), 2)
    look = iota((1, looks, planes * LANES), 1) - rest(over(lane, LANES), pieces) * looks_part
    spare = rest(lane, LANES) - look * LOOKC
    inside = (spare >= 0) & (spare < LOOKC)
    own_lane = over(iota((block, lanes), 1), looks) == iota((block, lanes), 0)

    def settle(chunk):
        arrived = parts[:, chunk].reshape(n_epoch * n_space * size, LANES)
        sorted_rows = jnp.dot(order[...], arrived, preferred_element_type=F32)
        many = MARGIN * total
        whole = [sorted_rows[p * many : (p + 1) * many] for p in range(planes)]
        re = jnp.concatenate(whole[:pieces], axis=1)
        im = jnp.concatenate(whole[pieces:], axis=1)
        plain = jnp.concatenate([re, im], axis=1)
        turned = jnp.concatenate([-im, re], axis=1)
        sums = jnp.dot(
            re * re + im * im,
            fold[...],
            preferred_element_type=F32,
            precision=lax.Precision.HIGHEST,
        )
        for n in range(MARGIN):
            row = chunk * MARGIN + n
            part_of = slice(n * total, (n + 1) * total)
            epochs[row] = plain[part_of]
            factor = jnp.concatenate([plain[part_of], turned[part_of]], axis=0)
            lefts[row] = factor.T.astype(BF16)
            folded[row] = sums[part_of]

    def place_of(group):
        first = group * block
        return pl.ds(pl.multiple_of(first, 8) if block % 8 == 0 else first, block)

    def gram(row, images):
        masked = jnp.where(inside, images[:, None, :], 0.0).astype(BF16)
        masked = masked.reshape(images.shape[0] * looks, planes * LANES)
        return jnp.dot(masked, lefts[row], preferred_element_type=F32)

    def add_up(terms):
        return functools.reduce(lambda p, q: p + q, terms)

    windows = [range(r, r + LOOKR) for r in range(strip)]
    known = held - MARGIN
    early = [r for r in range(strip) if r + LOOKR <= known]
    late = [r for r in range(strip) if r + LOOKR > known]
    halves = [(early[0], len(early)), (late[0], len(late))]

    def coh_copy(half, slot, to_i, source):
        start, count = halves[half]
        return pltpu.make_async_remote_copy(
            src_ref=coh.at[slot, pl.ds(start, count)],
            dst_ref=got.at[source, pl.ds(start, count)],
            send_sem=send_coh.at[half, slot],
            recv_sem=recv_coh.at[half, source],
            device_id={"epoch": to_i},
            device_id_type=MESH,
        )

    def finish(cross, r, to_i):
        power = add_up([folded[row] for row in windows[r]]) + 1e-06
        left = add_up([folded[row, place_of(to_i), :] for row in windows[r]]) + 1e-06
        left = jnp.sum(jnp.where(own_lane, left, 0.0), axis=0, keepdims=True)
        inverse = lax.rsqrt(left * power)
        cross = cross.T
        return jnp.concatenate(
            [cross[:total] * inverse, cross[total:] * inverse], axis=0
        ).astype(BF16)

    for half, (chunk_list, row_list) in enumerate(
        [
            (range(chunks - 1), range(known)),
            (range(chunks - 1, chunks), range(known, held)),
        ]
    ):
        for slot, (from_i, from_j) in enumerate(origins):
            by_place(
                half,
                my_j,
                lambda low, count: strip_copy(
                    half, slot, from_i, from_j, from_i * n_space + from_j, low, count
                ).wait_recv(),
            )
        for chunk in chunk_list:
            settle(chunk)
        for step in reversed(range(n_epoch)):
            to_i = epoch_peer(step)
            grams = {row: gram(row, epochs[row, place_of(to_i), :]) for row in row_list}
            for r in early if half == 0 else late:
                cross = add_up([grams[row] for row in windows[r] if row in grams])
                if half:
                    cross = cross + middle[to_i, r - late[0]]
                value = finish(cross, r, to_i)
                if step:
                    coh[step, r] = value
                else:
                    got[my_i, r] = value
            if step:
                coh_copy(half, step, to_i, my_i).start()
            if half == 0:
                for r in late:
                    middle[to_i, r - late[0]] = add_up(
                        [grams[row] for row in windows[r] if row in grams]
                    )

    for half in range(2):
        for step in reversed(range(1, n_epoch)):
            from_i = epoch_source(step)
            coh_copy(half, step, from_i, from_i).wait_recv()
    for half in range(2):
        for step in range(1, n_epoch):
            coh_copy(half, step, epoch_peer(step), my_i).wait_send()
        for slot, (to_i, to_j) in enumerate(targets):
            by_place(
                half,
                to_j,
                lambda low, count: strip_copy(
                    half, slot, to_i, to_j, me, low, count
                ).wait_send(),
            )


def spread_kernel(dims, got, out_hbm, out_ref, sem):
    n_epoch, block, total, strip, all_looks = dims
    looks = all_looks // n_epoch
    lanes = block * looks
    if lanes == LANES and (strip * n_epoch) % block == 0 and block & (block - 1) == 0:
        spot = over(iota((2 * total, lanes), 1), looks)
        copies = []
        for half in range(strip * n_epoch // block):
            tiles = []
            for t in range(half * block, (half + 1) * block):
                tiles.append(got[t % n_epoch, t // n_epoch].astype(F32))
            bit = 1
            while bit < block:
                low = spot & bit == 0
                turned_tiles = list(tiles)
                for t in range(block):
                    if t & bit:
                        continue
                    one, two = tiles[t], tiles[t + bit]
                    turned_tiles[t] = jnp.where(low, one, pltpu.roll(two, bit * looks, 1))
                    turned_tiles[t + bit] = jnp.where(
                        low, pltpu.roll(one, lanes - bit * looks, 1), two
                    )
                tiles = turned_tiles
                bit *= 2
            for e in range(block):
                value = tiles[e].astype(BF16)
                for k in range(2):
                    out_ref[k, e, :, half * lanes : (half + 1) * lanes] = value[
                        k * total : (k + 1) * total
                    ]
            side = pl.ds(half * lanes, lanes)
            copies.append(
                pltpu.make_async_copy(
                    out_ref.at[:, :, :, side], out_hbm.at[:, :, :, side], sem.at[half]
                )
            )
            copies[-1].start()
        for copy in copies:
            copy.wait()
    else:
        shape = (lanes, strip * all_looks)
        fro_e, fro_c, goal = iota(shape, 0) // looks, iota(shape, 0) % looks, iota(shape, 1)
        for e in range(block):

            def add(i, acc):
                for r in range(strip):
                    spread = one_hot((fro_e == e) & (goal == r * all_looks + i * looks + fro_c))
                    acc = acc + jnp.dot(got[i, r], spread, preferred_element_type=F32)
                return acc

            value = lax.fori_loop(0, n_epoch, add, jnp.zeros((2 * total, shape[1]), F32))
            value = value.astype(BF16)
            for k in range(2):
                out_ref[k, e] = value[k * total : (k + 1) * total]
        whole = pltpu.make_async_copy(out_ref, out_hbm, sem.at[0])
        whole.start()
        whole.wait()


def per_device(slc_stack):
    n_epoch, n_space = lax.axis_size("epoch"), lax.axis_size("space")
    _, local, rows, cols = slc_stack.shape
    strip = rows // n_space
    held = strip + 2 * MARGIN
    total = n_epoch * n_space * local
    block = n_space * local
    width = cols // n_epoch
    looks = width // LOOKC
    all_looks = cols // LOOKC
    lanes = block * looks
    pieces = next(p for p in range(1, looks + 1) if looks % p == 0 and width // p <= LANES)
    planes = 2 * pieces
    size = -(-MARGIN * local * planes // 16) * 16
    chunks = held // MARGIN
    sources = n_epoch * n_space
    dims = (n_epoch, n_space, local, rows, cols, strip, pieces, size)
    vmem = pl.BlockSpec(memory_space=pltpu.VMEM)
    hbm = pl.BlockSpec(memory_space=pl.ANY)
    got = pl.pallas_call(
        functools.partial(kernel, dims),
        out_shape=jax.ShapeDtypeStruct((n_epoch, strip, 2 * total, lanes), BF16),
        in_specs=[hbm],
        out_specs=vmem,
        scratch_shapes=[
            pltpu.VMEM(slc_stack.shape, BF16),
            pltpu.VMEM((planes * local * rows, n_epoch * LANES), BF16),
            pltpu.VMEM((sources, chunks, size, LANES), BF16),
            pltpu.VMEM((sources, chunks, size, LANES), BF16),
            pltpu.VMEM((planes * MARGIN * total, sources * size), BF16),
            pltpu.VMEM((pieces * LANES, lanes), F32),
            pltpu.VMEM((held, planes * LANES, 2 * total), BF16),
            pltpu.VMEM((held, total, planes * LANES), F32),
            pltpu.VMEM((held, total, lanes), F32),
            pltpu.VMEM((n_epoch, MARGIN, lanes, 2 * total), F32),
            pltpu.VMEM((n_epoch, strip, 2 * total, lanes), BF16),
            pltpu.SemaphoreType.DMA(()),
            pltpu.SemaphoreType.DMA((2, sources - 1)),
            pltpu.SemaphoreType.DMA((2, sources)),
            pltpu.SemaphoreType.DMA((2, n_epoch)),
            pltpu.SemaphoreType.DMA((2, n_epoch)),
        ],
        compiler_params=pltpu.CompilerParams(
            collective_id=0, has_side_effects=True, vmem_limit_bytes=48 * 1024 * 1024
        ),
        cost_estimate=pl.CostEstimate(flops=10**9, bytes_accessed=10**6, transcendentals=0),
    )(pltpu.with_memory_space_constraint(slc_stack, pltpu.HBM))
    out = jax.ShapeDtypeStruct((2, block, total, strip * all_looks), BF16)
    return pl.pallas_call(
        functools.partial(spread_kernel, (n_epoch, block, total, strip, all_looks)),
        out_shape=out,
        in_specs=[vmem],
        out_specs=hbm,
        scratch_shapes=[
            pltpu.VMEM(out.shape, BF16),
            pltpu.SemaphoreType.DMA((max(1, strip * n_epoch // block),)),
        ],
        compiler_params=pltpu.CompilerParams(vmem_limit_bytes=32 * 1024 * 1024),
    )(got)


def solution(mesh):
    in_specs = (P(None, ("epoch", "space"), "groups", None),)
    out_specs = P(None, "epoch", None, ("groups", "space"))
    return jax.shard_map(
        per_device, mesh=mesh, in_specs=in_specs, out_specs=out_specs, check_vma=False
    )
```

```python
import functools

import jax
import jax.numpy as jnp
from jax import lax
from jax.experimental import pallas as pl
from jax.experimental.pallas import tpu as pltpu
from jax.sharding import PartitionSpec as P

LOOKR = 5
LOOKC = 15
MARGIN = 2
LANES = 128
MESH = pl.DeviceIdType.MESH
F32 = jnp.float32
BF16 = jnp.bfloat16


def iota(shape, axis):
    return lax.broadcasted_iota(jnp.int32, shape, axis)


def one_hot(hits):
    return jnp.where(hits, 1.0, 0.0).astype(BF16)


def over(value, by):
    return value >> (by.bit_length() - 1) if by & (by - 1) == 0 else lax.div(value, by)


def rest(value, by):
    return value & (by - 1) if by & (by - 1) == 0 else lax.rem(value, by)


def kernel(dims, x_hbm, got, x_ref, cut, strips, parts, *rest_refs):
    n_epoch, n_space, local, rows, cols, strip, pieces, size = dims
    order, fold, lefts, epochs, folded, middle, coh = rest_refs[:7]
    load, send_strip, recv_strip, send_coh, recv_coh = rest_refs[7:]
    total = n_epoch * n_space * local
    block = n_space * local
    held = strip + 2 * MARGIN
    chunks = held // MARGIN
    width = cols // n_epoch
    part = width // pieces
    looks = width // LOOKC
    looks_part = looks // pieces
    planes = 2 * pieces
    lanes = block * looks
    my_i = lax.axis_index("epoch")
    my_j = lax.axis_index("space")
    me = my_i * n_space + my_j

    def epoch_peer(step):
        core = lax.rem(my_i + lax.rem(step, 2), 2)
        return lax.rem(lax.div(my_i, 2) + lax.div(step, 2), n_epoch // 2) * 2 + core

    def epoch_source(step):
        core = lax.rem(my_i + lax.rem(step, 2), 2)
        pair = lax.div(my_i, 2) + n_epoch // 2 - lax.div(step, 2)
        return lax.rem(pair, n_epoch // 2) * 2 + core

    others = n_epoch * n_space - 1

    def target(slot):
        step = others - slot
        a, b = lax.rem(step, n_epoch), lax.div(step, n_epoch)
        return epoch_peer(a), lax.rem(my_j + b, n_space)

    def origin(slot):
        step = others - slot
        a, b = lax.rem(step, n_epoch), lax.div(step, n_epoch)
        return epoch_source(a), lax.rem(my_j + n_space - b, n_space)

    loading = pltpu.make_async_copy(x_hbm, x_ref, load)
    loading.start()
    barrier = pltpu.get_barrier_semaphore()

    @pl.loop(0, others)
    def _(slot):
        to_i, to_j = target(slot)
        pl.semaphore_signal(
            barrier,
            inc=1,
            device_id={"epoch": to_i, "space": to_j},
            device_id_type=MESH,
        )

    shape = (n_space * chunks * size, planes * local * rows)
    goal, held_at = iota(shape, 0), iota(shape, 1)
    spot = rest(goal, size)
    row = over(spot, planes * local)
    first = over(goal, chunks * size) * strip - MARGIN
    wanted = first + rest(over(goal, size), chunks) * MARGIN + row
    pick = one_hot(
        (row < MARGIN)
        & (rest(spot, planes) == over(held_at, local * rows))
        & (rest(over(spot, planes), local) == rest(over(held_at, rows), local))
        & (wanted == rest(held_at, rows))
    )
    loading.wait()
    for k in range(2):
        image = x_ref[k].reshape(local * rows, cols).astype(F32)
        for i in range(n_epoch):
            for h in range(pieces):
                start = i * width + h * part
                piece = image[:, start : start + part]
                if part < LANES:
                    blank = jnp.zeros((local * rows, LANES - part), F32)
                    piece = jnp.concatenate([piece, blank], axis=1)
                plane = k * pieces + h
                cut[
                    plane * local * rows : (plane + 1) * local * rows,
                    i * LANES : (i + 1) * LANES,
                ] = piece.astype(BF16)
    picked = jnp.dot(pick, cut[...], preferred_element_type=F32).astype(BF16)
    for i in range(n_epoch):
        side = slice(i * LANES, (i + 1) * LANES)
        for j in range(n_space):
            for z in range(chunks):
                start = (j * chunks + z) * size
                strips[i * n_space + j, z] = picked[start : start + size, side]

    pl.semaphore_wait(barrier, others)

    def strip_copy(part, slot, to_i, to_j, source, low, count):
        return pltpu.make_async_remote_copy(
            src_ref=strips.at[to_i * n_space + to_j, pl.ds(low, count)],
            dst_ref=parts.at[source, pl.ds(low, count)],
            send_sem=send_strip.at[part, slot],
            recv_sem=recv_strip.at[part, source],
            device_id={"epoch": to_i, "space": to_j},
            device_id_type=MESH,
        )

    def by_place(part, j, act):
        if part == 0:
            pl.when(j == 0)(lambda: act(1, chunks - 2))
            pl.when(j > 0)(lambda: act(0, chunks - 1))
        else:
            pl.when(j < n_space - 1)(lambda: act(chunks - 1, 1))

    for part_of in range(2):

        @pl.loop(0, others)
        def _(slot):
            to_i, to_j = target(slot)
            by_place(
                part_of,
                to_j,
                lambda low, count: strip_copy(
                    part_of, slot, to_i, to_j, me, low, count
                ).start(),
            )

    @pl.when(my_j == 0)
    def _():
        parts[:, 0] = jnp.zeros((n_epoch * n_space, size, LANES), BF16)

    @pl.when(my_j == n_space - 1)
    def _():
        parts[:, chunks - 1] = jnp.zeros((n_epoch * n_space, size, LANES), BF16)

    parts[me] = strips[me]

    shape = (planes * MARGIN * total, n_epoch * n_space * size)
    goal, fro = iota(shape, 0), iota(shape, 1)
    spot = rest(fro, size)
    row = over(spot, planes * local)
    epoch = over(fro, size) * local + rest(over(spot, planes), local)
    want = (rest(spot, planes) * MARGIN + row) * total + epoch
    order[...] = one_hot((row < MARGIN) & (goal == want))
    lane = iota((pieces * LANES, lanes), 0)
    look = rest(iota((pieces * LANES, lanes), 1), looks) - over(lane, LANES) * looks_part
    spare = rest(lane, LANES) - look * LOOKC
    fold[...] = jnp.where((spare >= 0) & (spare < LOOKC), 1.0, 0.0)
    lane = iota((1, looks, planes * LANES), 2)
    look = iota((1, looks, planes * LANES), 1) - rest(over(lane, LANES), pieces) * looks_part
    spare = rest(lane, LANES) - look * LOOKC
    inside = (spare >= 0) & (spare < LOOKC)
    own_lane = over(iota((block, lanes), 1), looks) == iota((block, lanes), 0)

    def settle(chunk):
        arrived = parts[:, chunk].reshape(n_epoch * n_space * size, LANES)
        sorted_rows = jnp.dot(order[...], arrived, preferred_element_type=F32)
        many = MARGIN * total
        whole = [sorted_rows[p * many : (p + 1) * many] for p in range(planes)]
        re = jnp.concatenate(whole[:pieces], axis=1)
        im = jnp.concatenate(whole[pieces:], axis=1)
        plain = jnp.concatenate([re, im], axis=1)
        turned = jnp.concatenate([-im, re], axis=1)
        sums = jnp.dot(
            re * re + im * im,
            fold[...],
            preferred_element_type=F32,
            precision=lax.Precision.HIGHEST,
        )
        for n in range(MARGIN):
            row = chunk * MARGIN + n
            part_of = slice(n * total, (n + 1) * total)
            epochs[row] = plain[part_of]
            factor = jnp.concatenate([plain[part_of], turned[part_of]], axis=0)
            lefts[row] = factor.T.astype(BF16)
            folded[row] = sums[part_of]

    def place_of(group):
        first = group * block
        return pl.ds(pl.multiple_of(first, 8) if block % 8 == 0 else first, block)

    def gram(row, images):
        masked = jnp.where(inside, images[:, None, :], 0.0).astype(BF16)
        masked = masked.reshape(images.shape[0] * looks, planes * LANES)
        return jnp.dot(masked, lefts[row], preferred_element_type=F32)

    def add_up(terms):
        return functools.reduce(lambda p, q: p + q, terms)

    windows = [range(r, r + LOOKR) for r in range(strip)]
    known = held - MARGIN
    early = [r for r in range(strip) if r + LOOKR <= known]
    late = [r for r in range(strip) if r + LOOKR > known]
    halves = [(early[0], len(early)), (late[0], len(late))]

    def coh_copy(half, slot, to_i, source):
        start, count = halves[half]
        return pltpu.make_async_remote_copy(
            src_ref=coh.at[slot, pl.ds(start, count)],
            dst_ref=got.at[source, pl.ds(start, count)],
            send_sem=send_coh.at[half, slot],
            recv_sem=recv_coh.at[half, source],
            device_id={"epoch": to_i},
            device_id_type=MESH,
        )

    def finish(cross, r, to_i):
        power = add_up([folded[row] for row in windows[r]]) + 1e-06
        left = add_up([folded[row, place_of(to_i), :] for row in windows[r]]) + 1e-06
        left = jnp.sum(jnp.where(own_lane, left, 0.0), axis=0, keepdims=True)
        inverse = lax.rsqrt(left * power)
        cross = cross.T
        return jnp.concatenate(
            [cross[:total] * inverse, cross[total:] * inverse], axis=0
        ).astype(BF16)

    for half, (chunk_list, row_list) in enumerate(
        [
            (range(chunks - 1), range(known)),
            (range(chunks - 1, chunks), range(known, held)),
        ]
    ):

        @pl.loop(0, others)
        def _(slot):
            from_i, from_j = origin(slot)
            by_place(
                half,
                my_j,
                lambda low, count: strip_copy(
                    half, slot, from_i, from_j, from_i * n_space + from_j, low, count
                ).wait_recv(),
            )
        pl.loop(chunk_list.start, chunk_list.stop)(settle)

        @pl.loop(0, n_epoch)
        def _(turn):
            step = n_epoch - 1 - turn
            to_i = epoch_peer(step)
            grams = {row: gram(row, epochs[row, place_of(to_i), :]) for row in row_list}
            for r in early if half == 0 else late:
                cross = add_up([grams[row] for row in windows[r] if row in grams])
                if half:
                    cross = cross + middle[to_i, r - late[0]]
                coh[step, r] = finish(cross, r, to_i)
            pl.when(step > 0)(lambda: coh_copy(half, step, to_i, my_i).start())
            if half == 0:
                for r in late:
                    middle[to_i, r - late[0]] = add_up(
                        [grams[row] for row in windows[r] if row in grams]
                    )

    got[my_i] = coh[0]
    for half in range(2):

        @pl.loop(1, n_epoch)
        def _(step):
            from_i = epoch_source(step)
            coh_copy(half, step, from_i, from_i).wait_recv()
            coh_copy(half, step, epoch_peer(step), my_i).wait_send()

        @pl.loop(0, others)
        def _(slot):
            to_i, to_j = target(slot)
            by_place(
                half,
                to_j,
                lambda low, count: strip_copy(
                    half, slot, to_i, to_j, me, low, count
                ).wait_send(),
            )


def spread_kernel(dims, got, out_hbm, out_ref, sem):
    n_epoch, block, total, strip, all_looks = dims
    looks = all_looks // n_epoch
    lanes = block * looks
    if lanes == LANES and (strip * n_epoch) % block == 0 and block & (block - 1) == 0:
        spot = over(iota((2 * total, lanes), 1), looks)
        copies = []
        for half in range(strip * n_epoch // block):
            tiles = []
            for t in range(half * block, (half + 1) * block):
                tiles.append(got[t % n_epoch, t // n_epoch].astype(F32))
            bit = 1
            while bit < block:
                low = spot & bit == 0
                turned_tiles = list(tiles)
                for t in range(block):
                    if t & bit:
                        continue
                    one, two = tiles[t], tiles[t + bit]
                    turned_tiles[t] = jnp.where(low, one, pltpu.roll(two, bit * looks, 1))
                    turned_tiles[t + bit] = jnp.where(
                        low, pltpu.roll(one, lanes - bit * looks, 1), two
                    )
                tiles = turned_tiles
                bit *= 2
            for e in range(block):
                value = tiles[e].astype(BF16)
                for k in range(2):
                    out_ref[k, e, :, half * lanes : (half + 1) * lanes] = value[
                        k * total : (k + 1) * total
                    ]
            side = pl.ds(half * lanes, lanes)
            copies.append(
                pltpu.make_async_copy(
                    out_ref.at[:, :, :, side], out_hbm.at[:, :, :, side], sem.at[half]
                )
            )
            copies[-1].start()
        for copy in copies:
            copy.wait()
    else:
        shape = (lanes, strip * all_looks)
        fro_e, fro_c, goal = iota(shape, 0) // looks, iota(shape, 0) % looks, iota(shape, 1)
        for e in range(block):

            def add(i, acc):
                for r in range(strip):
                    spread = one_hot((fro_e == e) & (goal == r * all_looks + i * looks + fro_c))
                    acc = acc + jnp.dot(got[i, r], spread, preferred_element_type=F32)
                return acc

            value = lax.fori_loop(0, n_epoch, add, jnp.zeros((2 * total, shape[1]), F32))
            value = value.astype(BF16)
            for k in range(2):
                out_ref[k, e] = value[k * total : (k + 1) * total]
        whole = pltpu.make_async_copy(out_ref, out_hbm, sem.at[0])
        whole.start()
        whole.wait()


def per_device(slc_stack):
    n_epoch, n_space = lax.axis_size("epoch"), lax.axis_size("space")
    _, local, rows, cols = slc_stack.shape
    strip = rows // n_space
    held = strip + 2 * MARGIN
    total = n_epoch * n_space * local
    block = n_space * local
    width = cols // n_epoch
    looks = width // LOOKC
    all_looks = cols // LOOKC
    lanes = block * looks
    pieces = next(p for p in range(1, looks + 1) if looks % p == 0 and width // p <= LANES)
    planes = 2 * pieces
    size = -(-MARGIN * local * planes // 16) * 16
    chunks = held // MARGIN
    sources = n_epoch * n_space
    dims = (n_epoch, n_space, local, rows, cols, strip, pieces, size)
    vmem = pl.BlockSpec(memory_space=pltpu.VMEM)
    hbm = pl.BlockSpec(memory_space=pl.ANY)
    got = pl.pallas_call(
        functools.partial(kernel, dims),
        out_shape=jax.ShapeDtypeStruct((n_epoch, strip, 2 * total, lanes), BF16),
        in_specs=[hbm],
        out_specs=vmem,
        scratch_shapes=[
            pltpu.VMEM(slc_stack.shape, BF16),
            pltpu.VMEM((planes * local * rows, n_epoch * LANES), BF16),
            pltpu.VMEM((sources, chunks, size, LANES), BF16),
            pltpu.VMEM((sources, chunks, size, LANES), BF16),
            pltpu.VMEM((planes * MARGIN * total, sources * size), BF16),
            pltpu.VMEM((pieces * LANES, lanes), F32),
            pltpu.VMEM((held, planes * LANES, 2 * total), BF16),
            pltpu.VMEM((held, total, planes * LANES), F32),
            pltpu.VMEM((held, total, lanes), F32),
            pltpu.VMEM((n_epoch, MARGIN, lanes, 2 * total), F32),
            pltpu.VMEM((n_epoch, strip, 2 * total, lanes), BF16),
            pltpu.SemaphoreType.DMA(()),
            pltpu.SemaphoreType.DMA((2, sources - 1)),
            pltpu.SemaphoreType.DMA((2, sources)),
            pltpu.SemaphoreType.DMA((2, n_epoch)),
            pltpu.SemaphoreType.DMA((2, n_epoch)),
        ],
        compiler_params=pltpu.CompilerParams(
            collective_id=0, has_side_effects=True, vmem_limit_bytes=48 * 1024 * 1024
        ),
        cost_estimate=pl.CostEstimate(flops=10**9, bytes_accessed=10**6, transcendentals=0),
    )(pltpu.with_memory_space_constraint(slc_stack, pltpu.HBM))
    out = jax.ShapeDtypeStruct((2, block, total, strip * all_looks), BF16)
    return pl.pallas_call(
        functools.partial(spread_kernel, (n_epoch, block, total, strip, all_looks)),
        out_shape=out,
        in_specs=[vmem],
        out_specs=hbm,
        scratch_shapes=[
            pltpu.VMEM(out.shape, BF16),
            pltpu.SemaphoreType.DMA((max(1, strip * n_epoch // block),)),
        ],
        compiler_params=pltpu.CompilerParams(vmem_limit_bytes=32 * 1024 * 1024),
    )(got)


def solution(mesh):
    in_specs = (P(None, ("epoch", "space"), "groups", None),)
    out_specs = P(None, "epoch", None, ("groups", "space"))
    return jax.shard_map(
        per_device, mesh=mesh, in_specs=in_specs, out_specs=out_specs, check_vma=False
    )
```

```python
import functools

import jax
import jax.numpy as jnp
from jax import lax
from jax.experimental import pallas as pl
from jax.experimental.pallas import tpu as pltpu
from jax.sharding import PartitionSpec as P

LOOKR = 5
LOOKC = 15
MARGIN = 2
LANES = 128
MESH = pl.DeviceIdType.MESH
F32 = jnp.float32
BF16 = jnp.bfloat16


def iota(shape, axis):
    return lax.broadcasted_iota(jnp.int32, shape, axis)


def one_hot(hits):
    return jnp.where(hits, 1.0, 0.0).astype(BF16)


def over(value, by):
    return value >> (by.bit_length() - 1) if by & (by - 1) == 0 else lax.div(value, by)


def rest(value, by):
    return value & (by - 1) if by & (by - 1) == 0 else lax.rem(value, by)


def kernel(dims, x_hbm, got, x_ref, cut, mid_out, edge_out, mid_in, edge_in, *rest_refs):
    n_epoch, n_space, local, rows, cols, strip, pieces, mid_rows, edge_rows = dims
    mid_order, edge_order, fold, lefts, epochs, folded, middle, coh = rest_refs[:8]
    load, send_mid, recv_mid, send_edge, recv_edge, send_coh, recv_coh = rest_refs[8:]
    total = n_epoch * n_space * local
    block = n_space * local
    held = strip + 2 * MARGIN
    width = cols // n_epoch
    part = width // pieces
    looks = width // LOOKC
    looks_part = looks // pieces
    planes = 2 * pieces
    lanes = block * looks
    my_i = lax.axis_index("epoch")
    my_j = lax.axis_index("space")
    me = my_i * n_space + my_j

    def epoch_peer(step):
        core = lax.rem(lax.rem(my_i, 2) + step % 2, 2)
        return lax.rem(my_i // 2 + step // 2, n_epoch // 2) * 2 + core

    def epoch_source(step):
        core = lax.rem(lax.rem(my_i, 2) + step % 2, 2)
        return lax.rem(my_i // 2 + n_epoch // 2 - step // 2, n_epoch // 2) * 2 + core

    steps = [
        (a, b)
        for b in reversed(range(n_space))
        for a in reversed(range(n_epoch))
        if a or b
    ]
    targets = [(epoch_peer(a), lax.rem(my_j + b, n_space)) for a, b in steps]
    origins = [(epoch_source(a), lax.rem(my_j + n_space - b, n_space)) for a, b in steps]

    loading = [
        pltpu.make_async_copy(x_hbm.at[k, e], x_ref.at[k, e], load.at[k, e])
        for k in range(2)
        for e in range(local)
    ]
    for copy in loading:
        copy.start()
    barrier = pltpu.get_barrier_semaphore()
    for to_i, to_j in targets:
        pl.semaphore_signal(
            barrier,
            inc=1,
            device_id={"epoch": to_i, "space": to_j},
            device_id_type=MESH,
        )

    def picker(count, size, sides, first):
        shape = (n_space * sides * size, planes * local * rows)
        goal, held_at = iota(shape, 0), iota(shape, 1)
        spot = rest(goal, size)
        row = over(spot, planes * local)
        wanted = over(goal, sides * size) * strip + row + first(rest(over(goal, size), sides))
        return one_hot(
            (row < count)
            & (rest(spot, planes) == over(held_at, local * rows))
            & (rest(over(spot, planes), local) == rest(over(held_at, rows), local))
            & (wanted == rest(held_at, rows))
        )

    pick = jnp.concatenate(
        [
            picker(strip, mid_rows, 1, lambda side: 0),
            picker(
                MARGIN, edge_rows, 2, lambda side: jnp.where(side == 0, -MARGIN, strip)
            ),
        ],
        axis=0,
    )
    for copy in loading:
        copy.wait()
    for k in range(2):
        image = x_ref[k].reshape(local * rows, cols).astype(F32)
        for i in range(n_epoch):
            for h in range(pieces):
                start = i * width + h * part
                piece = image[:, start : start + part]
                if part < LANES:
                    blank = jnp.zeros((local * rows, LANES - part), F32)
                    piece = jnp.concatenate([piece, blank], axis=1)
                plane = k * pieces + h
                cut[
                    plane * local * rows : (plane + 1) * local * rows,
                    i * LANES : (i + 1) * LANES,
                ] = piece.astype(BF16)
    picked = jnp.dot(pick, cut[...], preferred_element_type=F32).astype(BF16)
    for i in range(n_epoch):
        side = slice(i * LANES, (i + 1) * LANES)
        for j in range(n_space):
            mid_out[i * n_space + j] = picked[j * mid_rows : (j + 1) * mid_rows, side]
            for z in range(2):
                start = n_space * mid_rows + (2 * j + z) * edge_rows
                edge_out[i * n_space + j, z] = picked[start : start + edge_rows, side]

    pl.semaphore_wait(barrier, len(steps))

    def mid_copy(slot, to_i, to_j, source):
        return pltpu.make_async_remote_copy(
            src_ref=mid_out.at[to_i * n_space + to_j],
            dst_ref=mid_in.at[source],
            send_sem=send_mid.at[slot],
            recv_sem=recv_mid.at[source],
            device_id={"epoch": to_i, "space": to_j},
            device_id_type=MESH,
        )

    def edge_copy(slot, to_i, to_j, source, low, count):
        return pltpu.make_async_remote_copy(
            src_ref=edge_out.at[to_i * n_space + to_j, pl.ds(low, count)],
            dst_ref=edge_in.at[source, pl.ds(low, count)],
            send_sem=send_edge.at[slot],
            recv_sem=recv_edge.at[source],
            device_id={"epoch": to_i, "space": to_j},
            device_id_type=MESH,
        )

    def by_place(j, act):
        if n_space > 1:
            pl.when(j == 0)(lambda: act(1, 1))
            pl.when(j == n_space - 1)(lambda: act(0, 1))
            pl.when((j > 0) & (j < n_space - 1))(lambda: act(0, 2))

    for slot, (to_i, to_j) in enumerate(targets):
        mid_copy(slot, to_i, to_j, me).start()
    for slot, (to_i, to_j) in enumerate(targets):
        by_place(
            to_j,
            lambda low, count: edge_copy(slot, to_i, to_j, me, low, count).start(),
        )

    @pl.when(my_j == 0)
    def _():
        edge_in[:, 0] = jnp.zeros((n_epoch * n_space, edge_rows, LANES), BF16)

    @pl.when(my_j == n_space - 1)
    def _():
        edge_in[:, 1] = jnp.zeros((n_epoch * n_space, edge_rows, LANES), BF16)

    mid_in[me] = mid_out[me]
    edge_in[me] = edge_out[me]

    def order(count, size):
        shape = (planes * count * total, n_epoch * n_space * size)
        goal, fro = iota(shape, 0), iota(shape, 1)
        spot = rest(fro, size)
        row = over(spot, planes * local)
        epoch = over(fro, size) * local + rest(over(spot, planes), local)
        want = (rest(spot, planes) * count + row) * total + epoch
        return one_hot((row < count) & (goal == want))

    mid_order[...] = order(strip, mid_rows)
    edge_order[...] = order(MARGIN, edge_rows)
    lane = iota((3 * pieces * LANES, lanes), 0)
    look = rest(iota(lane.shape, 1), looks) - rest(over(lane, LANES), pieces) * looks_part
    spare = rest(lane, LANES) - look * LOOKC
    fold[...] = one_hot((spare >= 0) & (spare < LOOKC))
    lane = iota((1, looks, planes * LANES), 2)
    look = iota((1, looks, planes * LANES), 1) - rest(over(lane, LANES), pieces) * looks_part
    spare = rest(lane, LANES) - look * LOOKC
    inside = (spare >= 0) & (spare < LOOKC)
    own_lane = over(iota((block, lanes), 1), looks) == iota((block, lanes), 0)

    def settle(order_ref, arrived, held_rows):
        count = len(held_rows)
        sorted_rows = jnp.dot(order_ref[...], arrived, preferred_element_type=F32)
        size = count * total
        whole = [sorted_rows[p * size : (p + 1) * size] for p in range(planes)]
        re = jnp.concatenate(whole[:pieces], axis=1)
        im = jnp.concatenate(whole[pieces:], axis=1)
        plain = jnp.concatenate([re, im], axis=1)
        turned = jnp.concatenate([-im, re], axis=1).astype(BF16)
        packed = plain.astype(BF16)
        square = re * re + im * im
        high = square.astype(BF16)
        left_over = square - high.astype(F32)
        mid = left_over.astype(BF16)
        low = (left_over - mid.astype(F32)).astype(BF16)
        terms = jnp.concatenate([high, mid, low], axis=1)
        sums = jnp.dot(terms, fold[...], preferred_element_type=F32)
        for n, row in enumerate(held_rows):
            part_of = slice(n * total, (n + 1) * total)
            epochs[row] = plain[part_of]
            lefts[row, :total] = packed[part_of]
            lefts[row, total:] = turned[part_of]
            folded[row] = sums[part_of]

    def place_of(group):
        first = group * block
        return pl.ds(pl.multiple_of(first, 8) if block % 8 == 0 else first, block)

    def gram(row, group):
        masked = jnp.where(inside, epochs[row, place_of(group), :][:, None, :], 0.0)
        return lax.dot_general(
            lefts[row],
            masked.astype(BF16).reshape(lanes, planes * LANES),
            (((1,), (1,)), ((), ())),
            preferred_element_type=F32,
        )

    def add_up(terms):
        return functools.reduce(lambda p, q: p + q, terms)

    own_rows = list(range(MARGIN, MARGIN + strip))
    edge_sides = [list(range(MARGIN)), list(range(MARGIN + strip, held))]
    windows = [range(r, r + LOOKR) for r in range(strip)]

    for slot, (from_i, from_j) in enumerate(origins):
        mid_copy(slot, from_i, from_j, from_i * n_space + from_j).wait_recv()
    settle(mid_order, mid_in[...].reshape(n_epoch * n_space * mid_rows, LANES), own_rows)
    for group in range(n_epoch):
        grams = {row: gram(row, group) for row in own_rows}
        for r in range(strip):
            middle[group, r] = add_up([grams[row] for row in windows[r] if row in grams])

    for slot, (from_i, from_j) in enumerate(origins):
        by_place(
            my_j,
            lambda low, count: edge_copy(
                slot, from_i, from_j, from_i * n_space + from_j, low, count
            ).wait_recv(),
        )
    for z in range(2):
        arrived = edge_in[:, z].reshape(n_epoch * n_space * edge_rows, LANES)
        settle(edge_order, arrived, edge_sides[z])

    def coh_copy(slot, to_i, source):
        return pltpu.make_async_remote_copy(
            src_ref=coh.at[slot],
            dst_ref=got.at[source],
            send_sem=send_coh.at[slot],
            recv_sem=recv_coh.at[source],
            device_id={"epoch": to_i},
            device_id_type=MESH,
        )

    for step in reversed(range(n_epoch)):
        to_i = epoch_peer(step)
        grams = {row: gram(row, to_i) for rows_of in edge_sides for row in rows_of}
        for r in range(strip):
            cross = middle[to_i, r] + add_up([grams[row] for row in windows[r] if row in grams])
            power = add_up([folded[row] for row in windows[r]]) + 1e-06
            left = add_up([folded[row, place_of(to_i), :] for row in windows[r]]) + 1e-06
            left = jnp.sum(jnp.where(own_lane, left, 0.0), axis=0, keepdims=True)
            inverse = lax.rsqrt(left * power)
            value = jnp.concatenate(
                [cross[:total] * inverse, cross[total:] * inverse], axis=0
            ).astype(BF16)
            if step:
                coh[step, r] = value
            else:
                got[my_i, r] = value
        if step:
            coh_copy(step, to_i, my_i).start()

    for step in reversed(range(1, n_epoch)):
        from_i = epoch_source(step)
        coh_copy(step, from_i, from_i).wait_recv()
    for step in range(1, n_epoch):
        coh_copy(step, epoch_peer(step), my_i).wait_send()
    for slot, (to_i, to_j) in enumerate(targets):
        mid_copy(slot, to_i, to_j, me).wait_send()
        by_place(
            to_j,
            lambda low, count: edge_copy(slot, to_i, to_j, me, low, count).wait_send(),
        )


def spread_kernel(dims, got, out_hbm, out_ref, sem):
    n_epoch, block, total, strip, all_looks = dims
    looks = all_looks // n_epoch
    lanes = block * looks
    if lanes == LANES and (strip * n_epoch) % block == 0 and block & (block - 1) == 0:
        spot = over(iota((2 * total, lanes), 1), looks)
        copies = []
        for half in range(strip * n_epoch // block):
            tiles = []
            for t in range(half * block, (half + 1) * block):
                tiles.append(got[t % n_epoch, t // n_epoch].astype(F32))
            bit = 1
            while bit < block:
                low = spot & bit == 0
                turned_tiles = list(tiles)
                for t in range(block):
                    if t & bit:
                        continue
                    one, two = tiles[t], tiles[t + bit]
                    turned_tiles[t] = jnp.where(low, one, pltpu.roll(two, bit * looks, 1))
                    turned_tiles[t + bit] = jnp.where(
                        low, pltpu.roll(one, lanes - bit * looks, 1), two
                    )
                tiles = turned_tiles
                bit *= 2
            for e in range(block):
                value = tiles[e].astype(BF16)
                for k in range(2):
                    out_ref[k, e, :, half * lanes : (half + 1) * lanes] = value[
                        k * total : (k + 1) * total
                    ]
                side = pl.ds(half * lanes, lanes)
                copies.append(
                    pltpu.make_async_copy(
                        out_ref.at[:, e, :, side],
                        out_hbm.at[:, e, :, side],
                        sem.at[half * block + e],
                    )
                )
                copies[-1].start()
        for copy in copies:
            copy.wait()
    else:
        shape = (lanes, strip * all_looks)
        fro_e, fro_c, goal = iota(shape, 0) // looks, iota(shape, 0) % looks, iota(shape, 1)
        for e in range(block):

            def add(i, acc):
                for r in range(strip):
                    spread = one_hot((fro_e == e) & (goal == r * all_looks + i * looks + fro_c))
                    acc = acc + jnp.dot(got[i, r], spread, preferred_element_type=F32)
                return acc

            value = lax.fori_loop(0, n_epoch, add, jnp.zeros((2 * total, shape[1]), F32))
            value = value.astype(BF16)
            for k in range(2):
                out_ref[k, e] = value[k * total : (k + 1) * total]
        whole = pltpu.make_async_copy(out_ref, out_hbm, sem.at[0])
        whole.start()
        whole.wait()


def per_device(slc_stack):
    n_epoch, n_space = lax.axis_size("epoch"), lax.axis_size("space")
    _, local, rows, cols = slc_stack.shape
    strip = rows // n_space
    held = strip + 2 * MARGIN
    total = n_epoch * n_space * local
    block = n_space * local
    width = cols // n_epoch
    looks = width // LOOKC
    all_looks = cols // LOOKC
    lanes = block * looks
    pieces = next(p for p in range(1, looks + 1) if looks % p == 0 and width // p <= LANES)
    planes = 2 * pieces
    mid_rows = -(-strip * local * planes // 16) * 16
    edge_rows = -(-MARGIN * local * planes // 16) * 16
    sources = n_epoch * n_space
    dims = (n_epoch, n_space, local, rows, cols, strip, pieces, mid_rows, edge_rows)
    vmem = pl.BlockSpec(memory_space=pltpu.VMEM)
    hbm = pl.BlockSpec(memory_space=pl.ANY)
    got = pl.pallas_call(
        functools.partial(kernel, dims),
        out_shape=jax.ShapeDtypeStruct((n_epoch, strip, 2 * total, lanes), BF16),
        in_specs=[hbm],
        out_specs=vmem,
        scratch_shapes=[
            pltpu.VMEM(slc_stack.shape, BF16),
            pltpu.VMEM((planes * local * rows, n_epoch * LANES), BF16),
            pltpu.VMEM((sources, mid_rows, LANES), BF16),
            pltpu.VMEM((sources, 2, edge_rows, LANES), BF16),
            pltpu.VMEM((sources, mid_rows, LANES), BF16),
            pltpu.VMEM((sources, 2, edge_rows, LANES), BF16),
            pltpu.VMEM((planes * strip * total, sources * mid_rows), BF16),
            pltpu.VMEM((planes * MARGIN * total, sources * edge_rows), BF16),
            pltpu.VMEM((3 * pieces * LANES, lanes), BF16),
            pltpu.VMEM((held, 2 * total, planes * LANES), BF16),
            pltpu.VMEM((held, total, planes * LANES), F32),
            pltpu.VMEM((held, total, lanes), F32),
            pltpu.VMEM((n_epoch, strip, 2 * total, lanes), F32),
            pltpu.VMEM((n_epoch, strip, 2 * total, lanes), BF16),
            pltpu.SemaphoreType.DMA((2, local)),
            pltpu.SemaphoreType.DMA((sources - 1,)),
            pltpu.SemaphoreType.DMA((sources,)),
            pltpu.SemaphoreType.DMA((sources - 1,)),
            pltpu.SemaphoreType.DMA((sources,)),
            pltpu.SemaphoreType.DMA((n_epoch,)),
            pltpu.SemaphoreType.DMA((n_epoch,)),
        ],
        compiler_params=pltpu.CompilerParams(
            collective_id=0, has_side_effects=True, vmem_limit_bytes=48 * 1024 * 1024
        ),
        cost_estimate=pl.CostEstimate(flops=10**9, bytes_accessed=10**6, transcendentals=0),
    )(pltpu.with_memory_space_constraint(slc_stack, pltpu.HBM))
    out = jax.ShapeDtypeStruct((2, block, total, strip * all_looks), BF16)
    return pl.pallas_call(
        functools.partial(spread_kernel, (n_epoch, block, total, strip, all_looks)),
        out_shape=out,
        in_specs=[vmem],
        out_specs=hbm,
        scratch_shapes=[
            pltpu.VMEM(out.shape, BF16),
            pltpu.SemaphoreType.DMA((strip * n_epoch,)),
        ],
        compiler_params=pltpu.CompilerParams(vmem_limit_bytes=32 * 1024 * 1024),
    )(got)


def solution(mesh):
    in_specs = (P(None, ("epoch", "space"), "groups", None),)
    out_specs = P(None, "epoch", None, ("groups", "space"))
    return jax.shard_map(
        per_device, mesh=mesh, in_specs=in_specs, out_specs=out_specs, check_vma=False
    )
```

```python
import functools

import jax
import jax.numpy as jnp
from jax import lax
from jax.experimental import pallas as pl
from jax.experimental.pallas import tpu as pltpu
from jax.sharding import PartitionSpec as P

LOOKR = 5
LOOKC = 15
MARGIN = 2
LANES = 128
MESH = pl.DeviceIdType.MESH
F32 = jnp.float32
BF16 = jnp.bfloat16


def iota(shape, axis):
    return lax.broadcasted_iota(jnp.int32, shape, axis)


def one_hot(hits):
    return jnp.where(hits, 1.0, 0.0).astype(BF16)


def over(value, by):
    return value >> (by.bit_length() - 1) if by & (by - 1) == 0 else lax.div(value, by)


def rest(value, by):
    return value & (by - 1) if by & (by - 1) == 0 else lax.rem(value, by)


def kernel(dims, x_hbm, got, x_ref, cut, mid_out, edge_out, mid_in, edge_in, *rest_refs):
    n_epoch, n_space, local, rows, cols, strip, pieces, mid_rows, edge_rows = dims
    mid_order, edge_order, fold, lefts, epochs, folded, middle, coh = rest_refs[:8]
    load, send_mid, recv_mid, send_edge, recv_edge, send_coh, recv_coh = rest_refs[8:]
    total = n_epoch * n_space * local
    block = n_space * local
    held = strip + 2 * MARGIN
    width = cols // n_epoch
    part = width // pieces
    looks = width // LOOKC
    looks_part = looks // pieces
    planes = 2 * pieces
    lanes = block * looks
    my_i = lax.axis_index("epoch")
    my_j = lax.axis_index("space")
    me = my_i * n_space + my_j

    def epoch_peer(step):
        core = lax.rem(lax.rem(my_i, 2) + step % 2, 2)
        return lax.rem(my_i // 2 + step // 2, n_epoch // 2) * 2 + core

    def epoch_source(step):
        core = lax.rem(lax.rem(my_i, 2) + step % 2, 2)
        return lax.rem(my_i // 2 + n_epoch // 2 - step // 2, n_epoch // 2) * 2 + core

    steps = [
        (a, b)
        for b in reversed(range(n_space))
        for a in reversed(range(n_epoch))
        if a or b
    ]
    near = n_space // 2 if n_space % 2 == 0 else n_space

    def space_peer(step):
        side = lax.rem(my_j // near + step // near, n_space // near)
        return side * near + lax.rem(lax.rem(my_j, near) + step % near, near)

    def space_source(step):
        side = lax.rem(my_j // near + step // near, n_space // near)
        return side * near + lax.rem(lax.rem(my_j, near) + near - step % near, near)

    targets = [(epoch_peer(a), space_peer(b)) for a, b in steps]
    origins = [(epoch_source(a), space_source(b)) for a, b in steps]

    loading = pltpu.make_async_copy(x_hbm, x_ref, load)
    loading.start()
    barrier = pltpu.get_barrier_semaphore()
    for to_i, to_j in targets:
        pl.semaphore_signal(
            barrier,
            inc=1,
            device_id={"epoch": to_i, "space": to_j},
            device_id_type=MESH,
        )

    def picker(count, size, sides, first):
        shape = (n_space * sides * size, planes * local * rows)
        goal, held_at = iota(shape, 0), iota(shape, 1)
        spot = rest(goal, size)
        row = over(spot, planes * local)
        wanted = over(goal, sides * size) * strip + row + first(rest(over(goal, size), sides))
        return one_hot(
            (row < count)
            & (rest(spot, planes) == over(held_at, local * rows))
            & (rest(over(spot, planes), local) == rest(over(held_at, rows), local))
            & (wanted == rest(held_at, rows))
        )

    pick = jnp.concatenate(
        [
            picker(strip, mid_rows, 1, lambda side: 0),
            picker(
                MARGIN, edge_rows, 2, lambda side: jnp.where(side == 0, -MARGIN, strip)
            ),
        ],
        axis=0,
    )
    loading.wait()
    for k in range(2):
        image = x_ref[k].reshape(local * rows, cols).astype(F32)
        for i in range(n_epoch):
            for h in range(pieces):
                start = i * width + h * part
                piece = image[:, start : start + part]
                if part < LANES:
                    blank = jnp.zeros((local * rows, LANES - part), F32)
                    piece = jnp.concatenate([piece, blank], axis=1)
                plane = k * pieces + h
                cut[
                    plane * local * rows : (plane + 1) * local * rows,
                    i * LANES : (i + 1) * LANES,
                ] = piece.astype(BF16)
    picked = jnp.dot(pick, cut[...], preferred_element_type=F32).astype(BF16)
    for i in range(n_epoch):
        side = slice(i * LANES, (i + 1) * LANES)
        for j in range(n_space):
            mid_out[i * n_space + j] = picked[j * mid_rows : (j + 1) * mid_rows, side]
            for z in range(2):
                start = n_space * mid_rows + (2 * j + z) * edge_rows
                edge_out[i * n_space + j, z] = picked[start : start + edge_rows, side]

    pl.semaphore_wait(barrier, len(steps))

    def mid_copy(slot, to_i, to_j, source):
        return pltpu.make_async_remote_copy(
            src_ref=mid_out.at[to_i * n_space + to_j],
            dst_ref=mid_in.at[source],
            send_sem=send_mid.at[slot],
            recv_sem=recv_mid.at[source],
            device_id={"epoch": to_i, "space": to_j},
            device_id_type=MESH,
        )

    def edge_copy(slot, to_i, to_j, source, low, count):
        return pltpu.make_async_remote_copy(
            src_ref=edge_out.at[to_i * n_space + to_j, pl.ds(low, count)],
            dst_ref=edge_in.at[source, pl.ds(low, count)],
            send_sem=send_edge.at[slot],
            recv_sem=recv_edge.at[source],
            device_id={"epoch": to_i, "space": to_j},
            device_id_type=MESH,
        )

    def by_place(j, act):
        if n_space > 1:
            pl.when(j == 0)(lambda: act(1, 1))
            pl.when(j == n_space - 1)(lambda: act(0, 1))
            pl.when((j > 0) & (j < n_space - 1))(lambda: act(0, 2))

    for slot, (to_i, to_j) in enumerate(targets):
        mid_copy(slot, to_i, to_j, me).start()
    for slot, (to_i, to_j) in enumerate(targets):
        by_place(
            to_j,
            lambda low, count: edge_copy(slot, to_i, to_j, me, low, count).start(),
        )

    @pl.when(my_j == 0)
    def _():
        edge_in[:, 0] = jnp.zeros((n_epoch * n_space, edge_rows, LANES), BF16)

    @pl.when(my_j == n_space - 1)
    def _():
        edge_in[:, 1] = jnp.zeros((n_epoch * n_space, edge_rows, LANES), BF16)

    mid_in[me] = mid_out[me]
    edge_in[me] = edge_out[me]

    def order(count, size):
        shape = (planes * count * total, n_epoch * n_space * size)
        goal, fro = iota(shape, 0), iota(shape, 1)
        spot = rest(fro, size)
        row = over(spot, planes * local)
        epoch = over(fro, size) * local + rest(over(spot, planes), local)
        want = (rest(spot, planes) * count + row) * total + epoch
        return one_hot((row < count) & (goal == want))

    mid_order[...] = order(strip, mid_rows)
    edge_order[...] = order(MARGIN, edge_rows)
    lane = iota((pieces * LANES, lanes), 0)
    look = rest(iota((pieces * LANES, lanes), 1), looks) - over(lane, LANES) * looks_part
    spare = rest(lane, LANES) - look * LOOKC
    fold[...] = jnp.where((spare >= 0) & (spare < LOOKC), 1.0, 0.0)
    lane = iota((1, looks, planes * LANES), 2)
    look = iota((1, looks, planes * LANES), 1) - rest(over(lane, LANES), pieces) * looks_part
    spare = rest(lane, LANES) - look * LOOKC
    inside = (spare >= 0) & (spare < LOOKC)
    own_lane = over(iota((block, lanes), 1), looks) == iota((block, lanes), 0)

    def settle(order_ref, arrived, held_rows):
        count = len(held_rows)
        sorted_rows = jnp.dot(order_ref[...], arrived, preferred_element_type=F32)
        size = count * total
        whole = [sorted_rows[p * size : (p + 1) * size] for p in range(planes)]
        re = jnp.concatenate(whole[:pieces], axis=1)
        im = jnp.concatenate(whole[pieces:], axis=1)
        plain = jnp.concatenate([re, im], axis=1)
        turned = jnp.concatenate([-im, re], axis=1).astype(BF16)
        packed = plain.astype(BF16)
        sums = jnp.dot(
            re * re + im * im,
            fold[...],
            preferred_element_type=F32,
            precision=lax.Precision.HIGHEST,
        )
        for n, row in enumerate(held_rows):
            part_of = slice(n * total, (n + 1) * total)
            epochs[row] = plain[part_of]
            lefts[row, :total] = packed[part_of]
            lefts[row, total:] = turned[part_of]
            folded[row] = sums[part_of]

    def place_of(group):
        first = group * block
        return pl.ds(pl.multiple_of(first, 8) if block % 8 == 0 else first, block)

    def gram(row, group):
        masked = jnp.where(inside, epochs[row, place_of(group), :][:, None, :], 0.0)
        return lax.dot_general(
            lefts[row],
            masked.astype(BF16).reshape(lanes, planes * LANES),
            (((1,), (1,)), ((), ())),
            preferred_element_type=F32,
        )

    def add_up(terms):
        return functools.reduce(lambda p, q: p + q, terms)

    own_rows = list(range(MARGIN, MARGIN + strip))
    edge_sides = [list(range(MARGIN)), list(range(MARGIN + strip, held))]
    windows = [range(r, r + LOOKR) for r in range(strip)]

    for slot, (from_i, from_j) in enumerate(origins):
        mid_copy(slot, from_i, from_j, from_i * n_space + from_j).wait_recv()
    settle(mid_order, mid_in[...].reshape(n_epoch * n_space * mid_rows, LANES), own_rows)
    for group in range(n_epoch):
        grams = {row: gram(row, group) for row in own_rows}
        for r in range(strip):
            middle[group, r] = add_up([grams[row] for row in windows[r] if row in grams])

    for slot, (from_i, from_j) in enumerate(origins):
        by_place(
            my_j,
            lambda low, count: edge_copy(
                slot, from_i, from_j, from_i * n_space + from_j, low, count
            ).wait_recv(),
        )
    for z in range(2):
        arrived = edge_in[:, z].reshape(n_epoch * n_space * edge_rows, LANES)
        settle(edge_order, arrived, edge_sides[z])

    def coh_copy(slot, to_i, source):
        return pltpu.make_async_remote_copy(
            src_ref=coh.at[slot],
            dst_ref=got.at[source],
            send_sem=send_coh.at[slot],
            recv_sem=recv_coh.at[source],
            device_id={"epoch": to_i},
            device_id_type=MESH,
        )

    for step in reversed(range(n_epoch)):
        to_i = epoch_peer(step)
        grams = {row: gram(row, to_i) for rows_of in edge_sides for row in rows_of}
        for r in range(strip):
            cross = middle[to_i, r] + add_up([grams[row] for row in windows[r] if row in grams])
            power = add_up([folded[row] for row in windows[r]]) + 1e-06
            left = add_up([folded[row, place_of(to_i), :] for row in windows[r]]) + 1e-06
            left = jnp.sum(jnp.where(own_lane, left, 0.0), axis=0, keepdims=True)
            inverse = lax.rsqrt(left * power)
            value = jnp.concatenate(
                [cross[:total] * inverse, cross[total:] * inverse], axis=0
            ).astype(BF16)
            if step:
                coh[step, r] = value
            else:
                got[my_i, r] = value
        if step:
            coh_copy(step, to_i, my_i).start()

    for step in reversed(range(1, n_epoch)):
        from_i = epoch_source(step)
        coh_copy(step, from_i, from_i).wait_recv()
    for step in range(1, n_epoch):
        coh_copy(step, epoch_peer(step), my_i).wait_send()
    for slot, (to_i, to_j) in enumerate(targets):
        mid_copy(slot, to_i, to_j, me).wait_send()
        by_place(
            to_j,
            lambda low, count: edge_copy(slot, to_i, to_j, me, low, count).wait_send(),
        )


def spread_kernel(dims, got, out_hbm, out_ref, sem):
    n_epoch, block, total, strip, all_looks = dims
    looks = all_looks // n_epoch
    lanes = block * looks
    if lanes == LANES and (strip * n_epoch) % block == 0 and block & (block - 1) == 0:
        spot = over(iota((2 * total, lanes), 1), looks)
        copies = []
        for half in range(strip * n_epoch // block):
            tiles = []
            for t in range(half * block, (half + 1) * block):
                tiles.append(got[t % n_epoch, t // n_epoch].astype(F32))
            bit = 1
            while bit < block:
                low = spot & bit == 0
                turned_tiles = list(tiles)
                for t in range(block):
                    if t & bit:
                        continue
                    one, two = tiles[t], tiles[t + bit]
                    turned_tiles[t] = jnp.where(low, one, pltpu.roll(two, bit * looks, 1))
                    turned_tiles[t + bit] = jnp.where(
                        low, pltpu.roll(one, lanes - bit * looks, 1), two
                    )
                tiles = turned_tiles
                bit *= 2
            for e in range(block):
                value = tiles[e].astype(BF16)
                for k in range(2):
                    out_ref[k, e, :, half * lanes : (half + 1) * lanes] = value[
                        k * total : (k + 1) * total
                    ]
            side = pl.ds(half * lanes, lanes)
            copies.append(
                pltpu.make_async_copy(
                    out_ref.at[:, :, :, side], out_hbm.at[:, :, :, side], sem.at[half]
                )
            )
            copies[-1].start()
        for copy in copies:
            copy.wait()
    else:
        shape = (lanes, strip * all_looks)
        fro_e, fro_c, goal = iota(shape, 0) // looks, iota(shape, 0) % looks, iota(shape, 1)
        for e in range(block):

            def add(i, acc):
                for r in range(strip):
                    spread = one_hot((fro_e == e) & (goal == r * all_looks + i * looks + fro_c))
                    acc = acc + jnp.dot(got[i, r], spread, preferred_element_type=F32)
                return acc

            value = lax.fori_loop(0, n_epoch, add, jnp.zeros((2 * total, shape[1]), F32))
            value = value.astype(BF16)
            for k in range(2):
                out_ref[k, e] = value[k * total : (k + 1) * total]
        whole = pltpu.make_async_copy(out_ref, out_hbm, sem.at[0])
        whole.start()
        whole.wait()


def per_device(slc_stack):
    n_epoch, n_space = lax.axis_size("epoch"), lax.axis_size("space")
    _, local, rows, cols = slc_stack.shape
    strip = rows // n_space
    held = strip + 2 * MARGIN
    total = n_epoch * n_space * local
    block = n_space * local
    width = cols // n_epoch
    looks = width // LOOKC
    all_looks = cols // LOOKC
    lanes = block * looks
    pieces = next(p for p in range(1, looks + 1) if looks % p == 0 and width // p <= LANES)
    planes = 2 * pieces
    mid_rows = -(-strip * local * planes // 16) * 16
    edge_rows = -(-MARGIN * local * planes // 16) * 16
    sources = n_epoch * n_space
    dims = (n_epoch, n_space, local, rows, cols, strip, pieces, mid_rows, edge_rows)
    vmem = pl.BlockSpec(memory_space=pltpu.VMEM)
    hbm = pl.BlockSpec(memory_space=pl.ANY)
    got = pl.pallas_call(
        functools.partial(kernel, dims),
        out_shape=jax.ShapeDtypeStruct((n_epoch, strip, 2 * total, lanes), BF16),
        in_specs=[hbm],
        out_specs=vmem,
        scratch_shapes=[
            pltpu.VMEM(slc_stack.shape, BF16),
            pltpu.VMEM((planes * local * rows, n_epoch * LANES), BF16),
            pltpu.VMEM((sources, mid_rows, LANES), BF16),
            pltpu.VMEM((sources, 2, edge_rows, LANES), BF16),
            pltpu.VMEM((sources, mid_rows, LANES), BF16),
            pltpu.VMEM((sources, 2, edge_rows, LANES), BF16),
            pltpu.VMEM((planes * strip * total, sources * mid_rows), BF16),
            pltpu.VMEM((planes * MARGIN * total, sources * edge_rows), BF16),
            pltpu.VMEM((pieces * LANES, lanes), F32),
            pltpu.VMEM((held, 2 * total, planes * LANES), BF16),
            pltpu.VMEM((held, total, planes * LANES), F32),
            pltpu.VMEM((held, total, lanes), F32),
            pltpu.VMEM((n_epoch, strip, 2 * total, lanes), F32),
            pltpu.VMEM((n_epoch, strip, 2 * total, lanes), BF16),
            pltpu.SemaphoreType.DMA(()),
            pltpu.SemaphoreType.DMA((sources - 1,)),
            pltpu.SemaphoreType.DMA((sources,)),
            pltpu.SemaphoreType.DMA((sources - 1,)),
            pltpu.SemaphoreType.DMA((sources,)),
            pltpu.SemaphoreType.DMA((n_epoch,)),
            pltpu.SemaphoreType.DMA((n_epoch,)),
        ],
        compiler_params=pltpu.CompilerParams(
            collective_id=0, has_side_effects=True, vmem_limit_bytes=48 * 1024 * 1024
        ),
        cost_estimate=pl.CostEstimate(flops=10**9, bytes_accessed=10**6, transcendentals=0),
    )(pltpu.with_memory_space_constraint(slc_stack, pltpu.HBM))
    out = jax.ShapeDtypeStruct((2, block, total, strip * all_looks), BF16)
    return pl.pallas_call(
        functools.partial(spread_kernel, (n_epoch, block, total, strip, all_looks)),
        out_shape=out,
        in_specs=[vmem],
        out_specs=hbm,
        scratch_shapes=[
            pltpu.VMEM(out.shape, BF16),
            pltpu.SemaphoreType.DMA((max(1, strip * n_epoch // block),)),
        ],
        compiler_params=pltpu.CompilerParams(vmem_limit_bytes=32 * 1024 * 1024),
    )(got)


def solution(mesh):
    in_specs = (P(None, ("epoch", "space"), "groups", None),)
    out_specs = P(None, "epoch", None, ("groups", "space"))
    return jax.shard_map(
        per_device, mesh=mesh, in_specs=in_specs, out_specs=out_specs, check_vma=False
    )
```
